32 devices in a mesh: section: 2 (over x), dp: 8 (over z, core), mp: 2 (over y).
Axes of the slice: x: 2, y: 2, z: 4, core: 2. Of those that a mesh axis runs over, the one named last changes fastest.
Arguments:
- frame_features: bfloat16 [3, 8192, 712], P(None, 'dp'), may hold values from -6 to 6
- clip_lengths: int32 [3, 8, 4], P(None, 'dp'), may hold values from 1 to 512, 768 in all within a row
- audio_drop: int32 [3, 8, 4], P(None, 'dp'), may hold values 0 or 1
- text_drop: int32 [3, 8, 4], P(None, 'dp'), may hold values 0 or 1
- timesteps: int32 [3, 8, 4], P(None, 'dp'), may hold values from 0 to 999
- cotangent: bfloat16 [3, 8192, 1024], P(None, ('dp', 'mp')), may hold values from -6 to 6
- embed_weight: bfloat16 [712, 1024], P(None, 'mp'), may hold values from -0.21875 to 0.21875
- embed_bias: bfloat16 [1024], P('mp'), may hold values from -1.75 to 1.75
- time_hidden_weight: bfloat16 [256, 1024], replicated, may hold values from -0.375 to 0.375
- time_hidden_bias: bfloat16 [1024], replicated, may hold values from -1.75 to 1.75
- time_output_weight: bfloat16 [1024, 1024], replicated, may hold values from -0.1875 to 0.1875
- time_output_bias: bfloat16 [1024], replicated, may hold values from -1.75 to 1.75
- modulate_weight: bfloat16 [2, 1024, 6, 1024], P('section', None, None, 'mp'), may hold values from -0.1875 to 0.1875
- modulate_bias: bfloat16 [2, 6, 1024], P('section', None, 'mp'), may hold values from -1.75 to 1.75
- project_weight: bfloat16 [2, 1024, 3, 1024], P('section', None, None, 'mp'), may hold values from -0.1875 to 0.1875
- project_bias: bfloat16 [2, 3, 1024], P('section', None, 'mp'), may hold values from -1.75 to 1.75
- output_weight: bfloat16 [2, 1024, 1024], P('section', 'mp'), may hold values from -2 to 2
- output_bias: bfloat16 [2, 1024], P('section'), may hold values from -1.75 to 1.75
- expand_weight: bfloat16 [2, 1024, 2048], P('section', None, 'mp'), may hold values from -0.1875 to 0.1875
- expand_bias: bfloat16 [2, 2048], P('section', 'mp'), may hold values from -1.75 to 1.75
- shrink_weight: bfloat16 [2, 2048, 1024], P('section', 'mp'), may hold values from -0.125 to 0.125
- shrink_bias: bfloat16 [2, 1024], P('section'), may hold values from -1.75 to 1.75
Outputs:
- stream: bfloat16 [2, 3, 8192, 1024], P('section', None, ('dp', 'mp'))
- stream_grad: float32 [2, 3, 8192, 1024], P('section', None, ('dp', 'mp'))
- embed_weight_grad: float32 [712, 1024], P(None, 'mp')
- embed_bias_grad: float32 [1024], P('mp')
- time_hidden_weight_grad: float32 [256, 1024], replicated
- time_hidden_bias_grad: float32 [1024], replicated
- time_output_weight_grad: float32 [1024, 1024], replicated
- time_output_bias_grad: float32 [1024], replicated
- modulate_weight_grad: float32 [2, 1024, 6, 1024], P('section', None, None, 'mp')
- modulate_bias_grad: float32 [2, 6, 1024], P('section', None, 'mp')
- project_weight_grad: float32 [2, 1024, 3, 1024], P('section', None, None, 'mp')
- project_bias_grad: float32 [2, 3, 1024], P('section', None, 'mp')
- output_weight_grad: float32 [2, 1024, 1024], P('section', 'mp')
- output_bias_grad: float32 [2, 1024], P('section')
- expand_weight_grad: float32 [2, 1024, 2048], P('section', None, 'mp')
- expand_bias_grad: float32 [2, 2048], P('section', 'mp')
- shrink_weight_grad: float32 [2, 2048, 1024], P('section', 'mp')
- shrink_bias_grad: float32 [2, 1024], P('section')
The draws below stay inside these ranges and needn't reach their ends.
Inputs may be any that keep to these rules, and one draw needn't show every extreme that they name: `clip_lengths`: each buffer's 4 lengths sum to 768; the last 256 frames are padding; one clip of every buffer has 512 frames.
All inputs are finite; a program needn't handle non-finite values. No bound on the sum of `audio_drop` or of `text_drop` on one device may be relied on, other than what follows from the above.
Results may differ from the reference program's by a relative error of at most 0.015.
Values may be sent and summed in bfloat16 or wider, within the bound.
A program may use at most 512 MiB of HBM per device.

```python
import math
import jax
import jax.numpy as jnp
import numpy as np
from jax import lax

D = 1024
HEADS = 16
HEAD = 64
FF = 2048
MEL = 100
FREQ = 256
FRAMES = 1024
CLIPS = 4
MB = 3
EMB_IN = 712
LIVE = 768
LONGEST = 512
SECTIONS = 2
N_DP = 8


def touch_ends(values, stream_key, least, high):
    shape = values.shape
    index_at = [jax.random.randint(jax.random.fold_in(stream_key, axis), (), 0, shape[axis]) for axis in range(len(shape))]
    values = values.at[tuple(index_at)].set(least)
    longest = shape.index(max(shape))
    index_at[longest] = (index_at[longest] + 1) % shape[longest]
    return values.at[tuple(index_at)].set(high)


def block_scale(rng, extent, cuts, smallest, largest):
    level = 1.0
    for axis_at, shards_of in cuts:
        steps = jax.random.uniform(jax.random.fold_in(jax.random.fold_in(rng, 6), axis_at), (shards_of,), jnp.float32, smallest / len(cuts), largest / len(cuts))
        level = level * jnp.repeat(jnp.exp(steps), extent[axis_at] // shards_of).reshape((-1,) + (1,) * (len(extent) - 1 - axis_at))
    return level


def profile(number_of, total, reach, skew):
    loads = [(1 << 20) // math.isqrt(grade ** skew) + 1 for grade in range(2, number_of + 1)]
    surplus, holding = total - reach - (number_of - 1), [1] * (number_of - 1)
    while surplus > 0:
        free = [i for i in range(number_of - 1) if holding[i] < reach]
        mass, budget = sum([loads[i] for i in free]), surplus
        for i in free:
            extra = min(reach - holding[i], max(1, budget * loads[i] // mass), surplus)
            holding[i] = holding[i] + extra
            surplus = surplus - extra
    return np.array([reach] + holding)


def ragged(rng, count, total, reach, skew):
    if count == 2:
        one = jax.random.randint(rng, (), max(1, total - reach), min(reach, total - 1) + 1)
        return jnp.stack([one, total - one])
    sizes = jnp.asarray(profile(count, total, reach, skew), jnp.int32)
    twos = (count - 1) // 2
    source_of, sink = sizes[1:1 + 2 * twos:2], sizes[2:2 + 2 * twos:2]
    room = jnp.minimum(source_of - 1, reach - sink)
    shifted = jax.random.randint(jax.random.fold_in(rng, 1), (twos,), 0, 1 << 20) % (room + 1)
    sizes = sizes.at[1:1 + 2 * twos:2].set(source_of - shifted).at[2:2 + 2 * twos:2].set(sink + shifted)
    return sizes[jax.random.permutation(jax.random.fold_in(rng, 2), count)]


def scatter_about(key, dims, scale, most, shards=(), kind=jnp.bfloat16):
    result = jax.random.normal(key, dims, jnp.float32) * scale
    if len(shards) > 0:
        result = block_scale(key, dims, shards, -0.22, 0.18) * result
    return jnp.clip(result, min=-most, max=most).astype(kind)


def setup_inputs(seed: int = 0) -> dict:
    seeds = jax.random.split(jax.random.key(seed), 23)
    return {
        "frame_features": scatter_about(seeds[0], (MB, N_DP * FRAMES, EMB_IN), 1.0, 6.0, ((1, 8),)),
        "clip_lengths": jax.vmap(lambda own: ragged(own, CLIPS, LIVE, LONGEST, 2))(jax.random.split(seeds[1], MB * N_DP)).reshape((MB, N_DP, CLIPS)).astype(jnp.int32),
        "audio_drop": touch_ends((jax.random.randint(seeds[2], (MB, N_DP, CLIPS), 0, 10) < 3).astype(jnp.int32), jax.random.fold_in(seeds[2], 1), 0, 1),
        "text_drop": touch_ends((jax.random.randint(seeds[3], (MB, N_DP, CLIPS), 0, 5) < 1).astype(jnp.int32), jax.random.fold_in(seeds[3], 1), 0, 1),
        "timesteps": touch_ends(jax.random.randint(seeds[4], (MB, N_DP, CLIPS), 0, 1000), jax.random.fold_in(seeds[4], 1), 0, 999).astype(jnp.int32),
        "cotangent": scatter_about(seeds[5], (MB, N_DP * FRAMES, D), 1.0, 6.0, ((1, 16),)),
        "embed_weight": scatter_about(seeds[6], (EMB_IN, D), EMB_IN ** -0.5, 0.21875, ((1, 2),)),
        "embed_bias": scatter_about(seeds[7], (D,), 0.3, 1.75, ((0, 2),)),
        "time_hidden_weight": scatter_about(seeds[8], (FREQ, D), FREQ ** -0.5, 0.375),
        "time_hidden_bias": scatter_about(seeds[9], (D,), 0.3, 1.75),
        "time_output_weight": scatter_about(seeds[10], (D, D), D ** -0.5, 0.1875),
        "time_output_bias": scatter_about(seeds[11], (D,), 0.3, 1.75),
        "modulate_weight": scatter_about(seeds[12], (SECTIONS, D, 6, D), D ** -0.5, 0.1875, ((0, 2), (3, 2))),
        "modulate_bias": scatter_about(seeds[13], (SECTIONS, 6, D), 0.3, 1.75, ((0, 2), (2, 2))),
        "project_weight": scatter_about(seeds[14], (SECTIONS, D, 3, D), D ** -0.5, 0.1875, ((0, 2), (3, 2))),
        "project_bias": scatter_about(seeds[15], (SECTIONS, 3, D), 0.3, 1.75, ((0, 2), (2, 2))),
        "output_weight": scatter_about(seeds[16], (SECTIONS, D, D), (max(D // 128, 8)) ** -0.5, 2.0, ((0, 2), (1, 2))),
        "output_bias": scatter_about(seeds[17], (SECTIONS, D), 0.3, 1.75, ((0, 2),)),
        "expand_weight": scatter_about(seeds[18], (SECTIONS, D, FF), D ** -0.5, 0.1875, ((0, 2), (2, 2))),
        "expand_bias": scatter_about(seeds[19], (SECTIONS, FF), 0.3, 1.75, ((0, 2), (1, 2))),
        "shrink_weight": scatter_about(seeds[20], (SECTIONS, FF, D), FF ** -0.5, 0.125, ((0, 2), (1, 2))),
        "shrink_bias": scatter_about(seeds[21], (SECTIONS, D), 0.3, 1.75, ((0, 2),)),
    }


precise = lax.Precision.HIGHEST
eps_norm = 1e-06
masked_score = -1e+30

@jax.custom_vjp
def low(v):
    return lax.optimization_barrier(v.astype(jnp.bfloat16)).astype(jnp.float32)

@jax.custom_vjp
def low_back(v):
    return v

def low_keep(v):
    return (low(v), None)

def low_pass(kept, grad):
    return (grad,)

def back_keep(v):
    return (v, None)

def back_low(kept, grad):
    return (low(grad),)
low.defvjp(low_keep, low_pass)
low_back.defvjp(back_keep, back_low)

def matmul(left, right):
    return jnp.dot(left, right, precision=precise, preferred_element_type=jnp.float32)

def clip_layout(lengths, frames):
    lengths = lengths.astype(jnp.int32)
    starts = (jnp.cumsum(lengths) - lengths).astype(jnp.int32)
    frame_index = jnp.arange(frames, dtype=jnp.int32)
    member = (frame_index[:, None] >= starts[None, :]) & (frame_index[:, None] < (starts + lengths)[None, :])
    onehot = member.astype(jnp.float32)
    alive_rows = lax.optimization_barrier(jnp.sum(onehot, 1))
    position = lax.optimization_barrier(jnp.sum(onehot * (frame_index[:, None] - starts[None, :]).astype(jnp.float32), 1))
    clip_ids = jnp.arange(lengths.shape[0], dtype=jnp.int32)
    member_count = lax.optimization_barrier(jnp.sum(member.astype(jnp.int32), 1)).astype(jnp.int32)
    segment = (lax.optimization_barrier(jnp.sum(member.astype(jnp.int32) * clip_ids[None, :], 1)) + (1 - member_count) * lengths.shape[0]).astype(jnp.int32)
    return (onehot, alive_rows, position, segment)

def rotate(values, position):
    half_count = values.shape[-1] // 2
    inverse = 1.0 / 10000.0 ** (jnp.arange(half_count, dtype=jnp.float32) * 2.0 / values.shape[-1])
    angles = position[:, None] * inverse[None, :]
    cosine = jnp.cos(angles)[:, None, :]
    sine_part = jnp.sin(angles)[:, None, :]
    paired = values.reshape(values.shape[:-1] + (half_count, 2))
    first_part = paired[..., 0]
    second_part = paired[..., 1]
    turned_first = first_part * cosine - second_part * sine_part
    turned_second = second_part * cosine + first_part * sine_part
    return jnp.stack([turned_first, turned_second], -1).reshape(values.shape)

def sinusoid(step_values, table_width):
    half_count = table_width // 2
    log_rate = math.log(10000.0) / (half_count - 1)
    frequency = jnp.exp(jnp.arange(half_count, dtype=jnp.float32) * -log_rate)
    angles = step_values.astype(jnp.float32)[:, None] * frequency[None, :]
    return jnp.concatenate([jnp.sin(angles), jnp.cos(angles)], 1)

def modulated_norm(stream, shift_part, scale_part):
    centered = stream - lax.optimization_barrier(jnp.mean(stream, -1, keepdims=True))
    variance = lax.optimization_barrier(jnp.mean(centered * centered, -1, keepdims=True))
    return centered * lax.rsqrt(variance + eps_norm) * (1.0 + scale_part) + shift_part

def attend(queries, key_heads, values, segment):
    frames = queries.shape[0]
    block_rows = min(512, frames)
    block_count = frames // block_rows
    score_scale = queries.shape[-1] ** (-0.5)

    def one_block(inputs):
        query_part, segment_part = inputs
        scores = low_back(jnp.einsum('qhd,khd->hqk', query_part, key_heads, precision=precise) * score_scale)
        allowed = segment_part[:, None] == segment[None, :]
        scores = jnp.where(allowed[None], scores, masked_score)
        row_max = lax.optimization_barrier(jnp.max(scores, -1, keepdims=True))
        weights = jnp.exp(scores - row_max)
        probabilities = weights / lax.optimization_barrier(jnp.sum(weights, -1, keepdims=True))
        return jnp.einsum('hqk,khd->qhd', low(probabilities), values, precision=precise)
    block_out = lax.map(jax.checkpoint(one_block), (queries.reshape(block_count, block_rows, queries.shape[1], queries.shape[2]), segment.reshape(block_count, block_rows)))
    return block_out.reshape(frames, queries.shape[1], queries.shape[2])

def layer(stream, token_mod, alive_rows, position, segment, weights):
    project_w, project_b, output_w, output_b, expand_w, expand_b, shrink_w, shrink_b = weights
    frames = stream.shape[0]
    normed = low(modulated_norm(stream, token_mod[:, 0], token_mod[:, 1]))
    projected = low_back(jnp.einsum('fd,dce->fce', normed, project_w, precision=precise) + project_b[None])
    queries = low(rotate(projected[:, 0].reshape(frames, HEADS, HEAD), position))
    key_heads = low(rotate(projected[:, 1].reshape(frames, HEADS, HEAD), position))
    values = low(projected[:, 2].reshape(frames, HEADS, HEAD))
    attended = low_back(low(attend(queries, key_heads, values, segment).reshape(frames, D)))
    branch = low_back(alive_rows[:, None] * (matmul(attended, output_w) + output_b[None]))
    stream = stream + token_mod[:, 2] * branch
    normed = low(modulated_norm(stream, token_mod[:, 3], token_mod[:, 4]))
    hidden = low(jax.nn.gelu(low_back(matmul(normed, expand_w) + expand_b[None]), approximate=True))
    return stream + token_mod[:, 5] * low_back(matmul(hidden, shrink_w) + shrink_b[None])

def one_buffer(params, inputs):
    embed_w, embed_b, hidden_w, hidden_b, output_tw, output_tb, modulate_w, modulate_b, project_w, project_b, output_w, output_b, expand_w, expand_b, shrink_w, shrink_b = params
    features, lengths, audio_off, text_off, step_values, entry_extra, middle_extra = inputs
    onehot, alive_rows, position, segment = clip_layout(lengths, FRAMES)
    audio_keep = matmul(onehot, (1 - audio_off).astype(jnp.float32))
    text_keep = matmul(onehot, (1 - text_off).astype(jnp.float32))
    column_index = jnp.arange(EMB_IN, dtype=jnp.int32)
    audio_columns = ((column_index >= MEL) & (column_index < 2 * MEL)).astype(jnp.float32)
    text_columns = (column_index >= 2 * MEL).astype(jnp.float32)
    factor = 1.0 - audio_columns - text_columns + audio_keep[:, None] * audio_columns[None, :] + text_keep[:, None] * text_columns[None, :]
    entry = low_back(low(matmul(features * factor, embed_w) + embed_b[None])) + entry_extra
    frequency_table = sinusoid(step_values, FREQ)
    time_embed = matmul(jax.nn.silu(matmul(frequency_table, hidden_w) + hidden_b[None]), output_tw) + output_tb[None]
    activated = jax.nn.silu(time_embed)
    stream = entry
    first_out = entry
    for section_index in range(2):
        modulation = jnp.einsum('cd,dje->cje', activated, modulate_w[section_index], precision=precise) + modulate_b[section_index][None]
        token_mod = jnp.einsum('fc,cje->fje', onehot, modulation, precision=precise)
        section_weights = (project_w[section_index], project_b[section_index], output_w[section_index], output_b[section_index], expand_w[section_index], expand_b[section_index], shrink_w[section_index], shrink_b[section_index])
        stream = layer(stream, token_mod, alive_rows, position, segment, section_weights)
        if section_index == 0:
            first_out = low(stream)
            stream = low_back(first_out) + middle_extra
    return (first_out, stream)

def reference(frame_features, clip_lengths, audio_drop, text_drop, timesteps, cotangent, embed_weight, embed_bias, time_hidden_weight, time_hidden_bias, time_output_weight, time_output_bias, modulate_weight, modulate_bias, project_weight, project_bias, output_weight, output_bias, expand_weight, expand_bias, shrink_weight, shrink_bias):
    buffers = MB * N_DP
    features = frame_features.astype(jnp.float32).reshape(buffers, FRAMES, EMB_IN)
    lengths = clip_lengths.reshape(buffers, CLIPS)
    audio_off = audio_drop.reshape(buffers, CLIPS)
    text_off = text_drop.reshape(buffers, CLIPS)
    step_values = timesteps.reshape(buffers, CLIPS)
    out_cot = cotangent.astype(jnp.float32).reshape(buffers, FRAMES, D)
    params = tuple([weight_array.astype(jnp.float32) for weight_array in (embed_weight, embed_bias, time_hidden_weight, time_hidden_bias, time_output_weight, time_output_bias, modulate_weight, modulate_bias, project_weight, project_bias, output_weight, output_bias, expand_weight, expand_bias, shrink_weight, shrink_bias)])
    zero_rows = jnp.zeros((buffers, FRAMES, D), jnp.float32)

    def forward(weight_set, entry_extra, middle_extra):

        def scan_step(carry_value, inputs):
            return (carry_value, jax.checkpoint(one_buffer)(weight_set, inputs))
        carry_value, outputs = lax.scan(scan_step, jnp.zeros((), jnp.float32), (features, lengths, audio_off, text_off, step_values, entry_extra, middle_extra))
        return outputs
    outputs, pullback = jax.vjp(forward, params, zero_rows, zero_rows)
    param_grads, entry_grad, middle_grad = pullback((jnp.zeros_like(outputs[0]), out_cot))
    stream = jnp.stack([outputs[0], outputs[1]]).astype(jnp.bfloat16).reshape(2, MB, N_DP * FRAMES, D)
    stream_grad = jnp.stack([entry_grad, middle_grad]).reshape(2, MB, N_DP * FRAMES, D)
    return (stream, stream_grad, param_grads[0], param_grads[1], param_grads[2], param_grads[3], param_grads[4], param_grads[5], param_grads[6], param_grads[7], param_grads[8], param_grads[9], param_grads[10], param_grads[11], param_grads[12], param_grads[13], param_grads[14], param_grads[15])
```

```python
import math

import jax
import jax.numpy as jnp
from jax import lax
from jax.experimental import pallas as pl
from jax.experimental.pallas import tpu as pltpu
from jax.sharding import Mesh
from jax.sharding import PartitionSpec as P

HEAD = 64
MEL = 100
LIVE = 768
LONGEST = 512
BLOCK = 256
LANES = 128
EPS = 1e-06
MASKED = -1e30
SCORE = math.log2(math.e) / math.sqrt(HEAD)
GELU = math.sqrt(2.0 / math.pi)

f32 = jnp.float32
bf16 = jnp.bfloat16
GROUP = ("section", "mp")
VMEM_LIMIT = 56 << 20


def dot_of(left, right, left_dim, right_dim):
    return lax.dot_general(
        left, right, (((left_dim,), (right_dim,)), ((), ())), preferred_element_type=f32
    )


def dot_nn(left, right):
    return dot_of(left, right, 1, 0)


def dot_nt(left, right):
    return dot_of(left, right, 1, 1)


def dot_tn(left, right):
    return dot_of(left, right, 0, 0)


def split_rows(values):
    high = values.astype(bf16)
    low = (values - high.astype(f32)).astype(bf16)
    return high, low


def dot_split(left, right):
    high, low = split_rows(left)
    both = dot_nn(jnp.concatenate([high, low], 0), right)
    rows = left.shape[0]
    return both[:rows] + both[rows:]


def whole_spec(value):
    rank = len(value.shape)
    return pl.BlockSpec(value.shape, lambda *_: (0,) * rank)


def any_spec():
    return pl.BlockSpec(memory_space=pl.ANY)


def smem_spec():
    return pl.BlockSpec(memory_space=pltpu.SMEM)


def shape_of(shape, kind):
    return jax.ShapeDtypeStruct(shape, kind)


def params_of(axes):
    return pltpu.CompilerParams(
        dimension_semantics=("arbitrary",) * axes, vmem_limit_bytes=VMEM_LIMIT
    )


def cost(flops, moved, special=0):
    return pl.CostEstimate(flops=int(flops), bytes_accessed=int(moved), transcendentals=int(special))


def start_fetch(place, refs, store, sems):
    parts, rows = store.shape[0], store.shape[1]
    if len(refs) == parts:
        for part in range(parts):
            pltpu.make_async_copy(refs[part], store.at[part], sems.at[part]).start()
        return
    own, mp_mine, mp_twin, sec_mine, sec_twin, far_mine, far_twin = refs
    half = rows // 2
    mine = pl.ds(pl.multiple_of(place[1] * half, half), half)
    twin = pl.ds(pl.multiple_of((1 - place[1]) * half, half), half)

    def halves(part, first, second):
        pltpu.make_async_copy(first, store.at[part, mine], sems.at[part]).start()
        pltpu.make_async_copy(second, store.at[part, twin], sems.at[part]).start()

    @pl.when(place[0] == 1)
    def _here():
        pltpu.make_async_copy(own, store.at[0], sems.at[0]).start()
        halves(1, mp_mine, mp_twin)

    @pl.when(place[0] != 1)
    def _there():
        halves(0, sec_mine, sec_twin)
        halves(1, far_mine, far_twin)


def wait_fetch(store, sems, part):
    pltpu.make_async_copy(store.at[part], store.at[part], sems.at[part]).wait()


def store_of(parts, rows, columns):
    return [pltpu.VMEM((parts, rows, columns), bf16), pltpu.SemaphoreType.DMA((parts,))]


def normal(rows):
    centered = rows - jnp.mean(rows, -1, keepdims=True)
    inverse = lax.rsqrt(jnp.mean(centered * centered, -1, keepdims=True) + EPS)
    return centered * inverse, inverse


def normal_back(unit, inverse, grad):
    return inverse * (
        grad
        - jnp.mean(grad, -1, keepdims=True)
        - unit * jnp.mean(grad * unit, -1, keepdims=True)
    )


def turn(values, cosine, sine):
    lane = lax.broadcasted_iota(jnp.int32, (values.shape[0], LANES), 1)
    even = lane % 2 == 0
    pieces = []
    for start in range(0, values.shape[1], LANES):
        piece = values[:, start : start + LANES]
        other = jnp.where(even, pltpu.roll(piece, LANES - 1, 1), pltpu.roll(piece, 1, 1))
        pieces.append(piece * cosine + other * sine)
    return pieces[0] if len(pieces) == 1 else jnp.concatenate(pieces, 1)


def gelu_parts(inner):
    square = inner * inner
    bend = jnp.tanh(GELU * inner * (1.0 + 0.044715 * square))
    half = 0.5 * (1.0 + bend)
    slope = half + 0.5 * inner * (1.0 - bend * bend) * (GELU * (1.0 + 0.134145 * square))
    return inner * half, slope


def project_kernel(place, x, one, mod, bias, cosine, sine, *rest):
    (normed, heads), (store, sems) = rest[-4:-2], rest[-2:]
    refs = rest[:-4]
    width = x.shape[1]
    columns = store.shape[2]
    step = pl.program_id(0)

    @pl.when(step == 0)
    def _start():
        start_fetch(place, refs, store, sems)

    shift_scale = dot_nn(one[...], mod[...])
    unit, _ = normal(x[...].astype(f32))
    rows = (unit * (1.0 + shift_scale[:, width:]) + shift_scale[:, :width]).astype(bf16)
    normed[...] = rows
    for part in range(store.shape[0]):

        @pl.when(step == 0)
        def _wait(part=part):
            wait_fetch(store, sems, part)

        for kind in range(3):
            out = dot_nn(rows, store[part, kind * width : (kind + 1) * width, :])
            out = out + bias[part, kind : kind + 1, :]
            if kind < 2:
                out = turn(out, cosine[...], sine[...])
            heads[part, kind] = out.astype(bf16)


def project(place, x, one, mod, bias, cosine, sine, refs, parts, columns):
    rows, width = x.shape
    row_block = lambda w: pl.BlockSpec((BLOCK, w), lambda i: (i, 0))
    return pl.pallas_call(
        project_kernel,
        grid=(rows // BLOCK,),
        in_specs=[
            smem_spec(),
            row_block(width),
            row_block(one.shape[1]),
            whole_spec(mod),
            whole_spec(bias),
            row_block(LANES),
            row_block(LANES),
        ]
        + [any_spec()] * len(refs),
        out_specs=[
            row_block(width),
            pl.BlockSpec((parts, 3, BLOCK, columns), lambda i: (0, 0, i, 0)),
        ],
        out_shape=[
            shape_of((rows, width), bf16),
            shape_of((parts, 3, rows, columns), bf16),
        ],
        scratch_shapes=store_of(parts, 3 * width, columns),
        compiler_params=params_of(1),
        cost_estimate=cost(6 * rows * width * columns * parts, 14 << 20),
        name="project",
    )(place, x, one, mod, bias, cosine, sine, *refs)


def attend_block(key, query, value, allowed):
    lane = lax.broadcasted_iota(jnp.int32, key.shape, 1)
    value_t = value.astype(f32).T.astype(bf16)
    outs, totals = [], []
    for head in range(2):
        mine = (lane < HEAD) if head == 0 else (lane >= HEAD)
        scores = dot_nt(jnp.where(mine, key, jnp.zeros_like(key)), query)
        if allowed is not None:
            scores = jnp.where(allowed, scores, MASKED)
        top = jnp.max(scores, 0, keepdims=True)
        weights = jnp.exp2((scores - top) * SCORE)
        total = jnp.sum(weights, 0, keepdims=True)
        out = dot_nn(value_t[head * HEAD : (head + 1) * HEAD], weights.astype(bf16))
        outs.append(out / total)
        totals.append(top * SCORE + jnp.log2(total))
    return jnp.concatenate(outs, 0).T, jnp.concatenate(totals, 0)


def attend_kernel(seg_row, seg_column, heads, attended, totals):
    allowed = seg_column[...] == seg_row[...]
    for rows, mask in ((pl.ds(0, LONGEST), None), (pl.ds(LONGEST, LIVE - LONGEST), allowed)):
        out, total = attend_block(heads[0, 1, rows], heads[0, 0, rows], heads[0, 2, rows], mask)
        attended[0, rows, :] = out.astype(bf16)
        totals[0, 0, :, rows] = total


def attend(seg_row, seg_column, heads):
    parts, _, rows, columns = heads.shape
    pairs = columns // LANES
    return pl.pallas_call(
        attend_kernel,
        grid=(parts, pairs),
        in_specs=[
            whole_spec(seg_row),
            whole_spec(seg_column),
            pl.BlockSpec((1, 3, rows, LANES), lambda i, j: (i, 0, 0, j)),
        ],
        out_specs=[
            pl.BlockSpec((1, rows, LANES), lambda i, j: (i, 0, j)),
            pl.BlockSpec((1, 1, 2, rows), lambda i, j: (i, j, 0, 0)),
        ],
        out_shape=[
            shape_of((parts, rows, columns), bf16),
            shape_of((parts, pairs, 2, rows), f32),
        ],
        compiler_params=params_of(2),
        cost_estimate=cost(8 << 30, 8 << 20),
        name="attend",
    )(seg_row, seg_column, heads)


def feed_kernel(place, x, attended, one, mod, out_bias, in_bias, shrink_bias, *rest):
    stores = rest[-6:]
    mid, branch_a, normed, inner, branch_f, x_out = rest[-12:-6]
    refs = rest[:-12]
    third = len(refs) // 3
    out_store, out_sems, in_store, in_sems, shrink_store, shrink_sems = stores
    parts = out_store.shape[0]
    width = x.shape[1]
    step = pl.program_id(0)

    @pl.when(step == 0)
    def _start():
        start_fetch(place, refs[:third], out_store, out_sems)
        start_fetch(place, refs[third : 2 * third], in_store, in_sems)
        start_fetch(place, refs[2 * third :], shrink_store, shrink_sems)

    def arrive(store, sems, part):
        @pl.when(step == 0)
        def _wait():
            wait_fetch(store, sems, part)

    token = dot_nn(one[...], mod[...])
    branch = out_bias[...]
    for part in range(parts):
        arrive(out_store, out_sems, part)
        branch = branch + dot_nn(attended[part], out_store[part])
    branch_a[...] = branch.astype(bf16)
    middle = x[...].astype(f32) + token[:, :width] * branch
    mid[...] = middle
    unit, _ = normal(middle)
    rows = (unit * (1.0 + token[:, 2 * width : 3 * width]) + token[:, width : 2 * width]).astype(bf16)
    normed[...] = rows
    hidden = []
    for part in range(parts):
        arrive(in_store, in_sems, part)
        act = dot_nn(rows, in_store[part]) + in_bias[part]
        inner[part] = act.astype(bf16)
        bend = jnp.tanh(GELU * act * (1.0 + 0.044715 * act * act))
        hidden.append((act * (0.5 + 0.5 * bend)).astype(bf16))
    branch = shrink_bias[...]
    for part in range(parts):
        arrive(shrink_store, shrink_sems, part)
        branch = branch + dot_nn(hidden[part], shrink_store[part])
    branch_f[...] = branch.astype(bf16)
    x_out[...] = (middle + token[:, 3 * width :] * branch).astype(bf16)


def feed(place, x, attended, one, mod, out_bias, in_bias, shrink_bias, out_refs, in_refs, shrink_refs):
    rows, width = x.shape
    parts, _, columns = attended.shape
    hidden = in_bias.shape[2]
    row_block = lambda w: pl.BlockSpec((BLOCK, w), lambda i: (i, 0))
    part_block = lambda w: pl.BlockSpec((parts, BLOCK, w), lambda i: (0, i, 0))
    return pl.pallas_call(
        feed_kernel,
        grid=(rows // BLOCK,),
        in_specs=[
            smem_spec(),
            row_block(width),
            part_block(columns),
            row_block(one.shape[1]),
            whole_spec(mod),
            whole_spec(out_bias),
            whole_spec(in_bias),
            whole_spec(shrink_bias),
        ]
        + [any_spec()] * (3 * len(out_refs)),
        out_specs=[
            row_block(width),
            row_block(width),
            row_block(width),
            part_block(hidden),
            row_block(width),
            row_block(width),
        ],
        out_shape=[
            shape_of((rows, width), f32),
            shape_of((rows, width), bf16),
            shape_of((rows, width), bf16),
            shape_of((parts, rows, hidden), bf16),
            shape_of((rows, width), bf16),
            shape_of((rows, width), bf16),
        ],
        scratch_shapes=store_of(parts, columns, width)
        + store_of(parts, width, hidden)
        + store_of(parts, hidden, width),
        compiler_params=params_of(1),
        cost_estimate=cost(2 * rows * width * parts * (columns + 2 * hidden), 24 << 20),
        name="feed",
    )(place, x, attended, one, mod, out_bias, in_bias, shrink_bias, *out_refs, *in_refs, *shrink_refs)


def feed_back_kernel(place, grad, inner, mid, branch_a, branch_f, one, mod, *rest):
    stores = rest[-6:]
    outs = rest[-15:-6]
    refs = rest[:-15]
    gf_out, hidden_out, dinner_out, ga_out, datt_out, gmid_out, dmod, row_sums, inner_sums = outs
    third = len(refs) // 3
    out_store, out_sems, in_store, in_sems, shrink_store, shrink_sems = stores
    parts = out_store.shape[0]
    width = grad.shape[1]
    step = pl.program_id(0)

    @pl.when(step == 0)
    def _start():
        start_fetch(place, refs[2 * third :], shrink_store, shrink_sems)
        start_fetch(place, refs[third : 2 * third], in_store, in_sems)
        start_fetch(place, refs[:third], out_store, out_sems)
        dmod[...] = jnp.zeros_like(dmod)
        row_sums[...] = jnp.zeros_like(row_sums)
        inner_sums[...] = jnp.zeros_like(inner_sums)

    def arrive(store, sems, part):
        @pl.when(step == 0)
        def _wait():
            wait_fetch(store, sems, part)

    token = dot_nn(one[...], mod[...])
    member = one[...]
    g = grad[...].astype(f32)
    gf = (token[:, 3 * width :] * g).astype(bf16)
    gf_out[...] = gf
    row_sums[0] += dot_tn(member, gf)
    dmod[3] += dot_tn(member, (g * branch_f[...].astype(f32)).astype(bf16))
    dnormed = None
    for part in range(parts):
        arrive(shrink_store, shrink_sems, part)
        dhidden = dot_nt(gf, shrink_store[part])
        value, slope = gelu_parts(inner[part].astype(f32))
        hidden_out[part] = value.astype(bf16)
        dinner = (slope * dhidden).astype(bf16)
        dinner_out[part] = dinner
        inner_sums[part] += dot_tn(member, dinner)
        arrive(in_store, in_sems, part)
        piece = dot_nt(dinner, in_store[part])
        dnormed = piece if dnormed is None else dnormed + piece
    unit, inverse = normal(mid[...])
    dmod[1] += dot_tn(member, dnormed.astype(bf16))
    dmod[2] += dot_tn(member, (dnormed * unit).astype(bf16))
    gmid = g + normal_back(unit, inverse, dnormed * (1.0 + token[:, 2 * width : 3 * width]))
    gmid_out[...] = gmid
    dmod[0] += dot_tn(member, (gmid * branch_a[...].astype(f32)).astype(bf16))
    ga = (token[:, :width] * gmid).astype(bf16)
    ga_out[...] = ga
    row_sums[1] += dot_tn(member, ga)
    for part in range(parts):
        arrive(out_store, out_sems, part)
        datt_out[part] = dot_nt(ga, out_store[part]).astype(bf16)


def feed_back(place, grad, inner, mid, branch_a, branch_f, one, mod, out_refs, in_refs, shrink_refs, columns):
    rows, width = grad.shape
    parts, _, hidden = inner.shape
    row_block = lambda w: pl.BlockSpec((BLOCK, w), lambda i: (i, 0))
    part_block = lambda w: pl.BlockSpec((parts, BLOCK, w), lambda i: (0, i, 0))
    clips = one.shape[1]
    fixed = lambda *shape: pl.BlockSpec(shape, lambda i: (0,) * len(shape))
    return pl.pallas_call(
        feed_back_kernel,
        grid=(rows // BLOCK,),
        in_specs=[
            smem_spec(),
            row_block(width),
            part_block(hidden),
            row_block(width),
            row_block(width),
            row_block(width),
            row_block(clips),
            whole_spec(mod),
        ]
        + [any_spec()] * (3 * len(out_refs)),
        out_specs=[
            row_block(width),
            part_block(hidden),
            part_block(hidden),
            row_block(width),
            part_block(columns),
            row_block(width),
            fixed(4, clips, width),
            fixed(2, clips, width),
            fixed(parts, clips, hidden),
        ],
        out_shape=[
            shape_of((rows, width), bf16),
            shape_of((parts, rows, hidden), bf16),
            shape_of((parts, rows, hidden), bf16),
            shape_of((rows, width), bf16),
            shape_of((parts, rows, columns), bf16),
            shape_of((rows, width), f32),
            shape_of((4, clips, width), f32),
            shape_of((2, clips, width), f32),
            shape_of((parts, clips, hidden), f32),
        ],
        scratch_shapes=store_of(parts, columns, width)
        + store_of(parts, width, hidden)
        + store_of(parts, hidden, width),
        compiler_params=params_of(1),
        cost_estimate=cost(2 * rows * width * parts * (columns + 2 * hidden), 32 << 20),
        name="feed_back",
    )(place, grad, inner, mid, branch_a, branch_f, one, mod, *out_refs, *in_refs, *shrink_refs)


def attend_back_block(key, query, value, out, dout, totals, allowed):
    lane = lax.broadcasted_iota(jnp.int32, key.shape, 1)
    out_t = out.astype(f32).T
    dout_t = dout.astype(f32).T
    key_t = key.astype(f32).T.astype(bf16)
    centres = out_t * dout_t
    dqueries, dkey, dvalue = [], None, None
    for head in range(2):
        mine = (lane < HEAD) if head == 0 else (lane >= HEAD)
        own = lambda array: jnp.where(mine, array, jnp.zeros_like(array))
        rows = slice(head * HEAD, (head + 1) * HEAD)
        scores = dot_nt(own(key), query)
        if allowed is not None:
            scores = jnp.where(allowed, scores, MASKED)
        weights = jnp.exp2(scores * SCORE - totals[head : head + 1])
        dweights = dot_nt(own(value), dout)
        centre = jnp.sum(centres[rows], 0, keepdims=True)
        dscores = (weights * (dweights - centre)).astype(bf16)
        piece = dot_nn(weights.astype(bf16), own(dout))
        dvalue = piece if dvalue is None else dvalue + piece
        piece = dot_nn(dscores, own(query))
        dkey = piece if dkey is None else dkey + piece
        dqueries.append(dot_nn(key_t[rows], dscores))
    scale = HEAD ** (-0.5)
    return jnp.concatenate(dqueries, 0).T * scale, dkey * scale, dvalue


def attend_back_kernel(seg_row, seg_column, cosine, sine, heads, attended, datt, totals, dheads):
    allowed = seg_column[...] == seg_row[...]
    for rows, mask in ((pl.ds(0, LONGEST), None), (pl.ds(LONGEST, LIVE - LONGEST), allowed)):
        dquery, dkey, dvalue = attend_back_block(
            heads[0, 1, rows],
            heads[0, 0, rows],
            heads[0, 2, rows],
            attended[0, rows],
            datt[0, rows],
            totals[0, 0, :, rows],
            mask,
        )
        dheads[0, 0, rows] = turn(dquery, cosine[rows], -sine[rows]).astype(bf16)
        dheads[0, 1, rows] = turn(dkey, cosine[rows], -sine[rows]).astype(bf16)
        dheads[0, 2, rows] = dvalue.astype(bf16)


def attend_back(seg_row, seg_column, cosine, sine, heads, attended, datt, totals):
    parts, _, rows, columns = heads.shape
    pairs = columns // LANES
    triple = pl.BlockSpec((1, 3, rows, LANES), lambda i, j: (i, 0, 0, j))
    single = pl.BlockSpec((1, rows, LANES), lambda i, j: (i, 0, j))
    return pl.pallas_call(
        attend_back_kernel,
        grid=(parts, pairs),
        in_specs=[
            whole_spec(seg_row),
            whole_spec(seg_column),
            whole_spec(cosine),
            whole_spec(sine),
            triple,
            single,
            single,
            pl.BlockSpec((1, 1, 2, rows), lambda i, j: (i, j, 0, 0)),
        ],
        out_specs=triple,
        out_shape=shape_of(heads.shape, bf16),
        compiler_params=params_of(2),
        cost_estimate=cost(16 << 30, 16 << 20),
        name="attend_back",
    )(seg_row, seg_column, cosine, sine, heads, attended, datt, totals)


def project_back_kernel(place, gmid, x, dheads, one, mod, *rest):
    store, sems = rest[-2:]
    gin, dmod, head_sums = rest[-5:-2]
    refs = rest[:-5]
    width = x.shape[1]
    step = pl.program_id(0)

    @pl.when(step == 0)
    def _start():
        start_fetch(place, refs, store, sems)
        dmod[...] = jnp.zeros_like(dmod)
        head_sums[...] = jnp.zeros_like(head_sums)

    member = one[...]
    dnormed = None
    for part in range(store.shape[0]):

        @pl.when(step == 0)
        def _wait(part=part):
            wait_fetch(store, sems, part)

        for kind in range(3):
            rows = dheads[part, kind]
            head_sums[part, kind] += dot_tn(member, rows)
            piece = dot_nt(rows, store[part, kind * width : (kind + 1) * width, :])
            dnormed = piece if dnormed is None else dnormed + piece
    scale = dot_nn(member, mod[...])
    unit, inverse = normal(x[...].astype(f32))
    dmod[0] += dot_tn(member, dnormed.astype(bf16))
    dmod[1] += dot_tn(member, (dnormed * unit).astype(bf16))
    gin[...] = (gmid[...] + normal_back(unit, inverse, dnormed * (1.0 + scale))).astype(bf16)


def project_back(place, gmid, x, dheads, one, mod, refs):
    rows, width = x.shape
    parts, _, _, columns = dheads.shape
    row_block = lambda w: pl.BlockSpec((BLOCK, w), lambda i: (i, 0))
    clips = one.shape[1]
    fixed = lambda *shape: pl.BlockSpec(shape, lambda i: (0,) * len(shape))
    return pl.pallas_call(
        project_back_kernel,
        grid=(rows // BLOCK,),
        in_specs=[
            smem_spec(),
            row_block(width),
            row_block(width),
            pl.BlockSpec((parts, 3, BLOCK, columns), lambda i: (0, 0, i, 0)),
            row_block(clips),
            whole_spec(mod),
        ]
        + [any_spec()] * len(refs),
        out_specs=[row_block(width), fixed(2, clips, width), fixed(parts, 3, clips, columns)],
        out_shape=[
            shape_of((rows, width), bf16),
            shape_of((2, clips, width), f32),
            shape_of((parts, 3, clips, columns), f32),
        ],
        scratch_shapes=store_of(parts, 3 * width, columns),
        compiler_params=params_of(1),
        cost_estimate=cost(6 * rows * width * columns * parts, 18 << 20),
        name="project_back",
    )(place, gmid, x, dheads, one, mod, *refs)


def weight_grad_split_kernel(core, left, right, send, keep):
    value = dot_tn(left[...].reshape(left.shape[-2:]), right[...].reshape(right.shape[-2:]))
    side = pl.program_id(0)

    @pl.when(side == 0)
    def _send():
        send[0] = value.astype(bf16)

    @pl.when(side == 1)
    def _keep():
        keep[0] = value.astype(bf16)


def weight_grad_kernel(left, right, out):
    value = dot_tn(left[...].reshape(left.shape[-2:]), right[...].reshape(right.shape[-2:]))
    out[0] = value.astype(bf16)


def weight_grad(core, left, right, parts):
    frames, columns = right.shape[-2:]
    kinds = right.shape[1] if right.ndim == 4 else 1
    left_rows = left.shape[-1]
    rows = kinds * left_rows
    estimate = cost(2 * frames * rows * columns * parts, 2 * parts * rows * columns + (6 << 20))
    if core is None:
        left_block = pl.BlockSpec(
            (1,) * (left.ndim - 2) + (frames, left_rows),
            (lambda p, k: (p, 0, 0)) if left.ndim == 3 else (lambda p, k: (0, 0)),
        )
        right_block = pl.BlockSpec(
            (1,) * (right.ndim - 2) + (frames, columns),
            {
                2: lambda p, k: (0, 0),
                3: lambda p, k: (p, 0, 0),
                4: lambda p, k: (p, k, 0, 0),
            }[right.ndim],
        )
        return pl.pallas_call(
            weight_grad_kernel,
            grid=(parts, kinds),
            in_specs=[left_block, right_block],
            out_specs=pl.BlockSpec((1, left_rows, columns), lambda p, k: (p, k, 0)),
            out_shape=shape_of((parts, rows, columns), bf16),
            compiler_params=params_of(2),
            cost_estimate=estimate,
            name="weight_grad",
        )(left, right)
    unit = left_rows // 2

    def unit_of(side, step, core_ref):
        half = jnp.where(side == 0, 1 - core_ref[0], core_ref[0])
        return half * kinds + step

    def left_map(side, part, step, core_ref):
        column = unit_of(side, step, core_ref) % 2
        return (part, 0, column) if left.ndim == 3 else (0, column)

    def right_map(side, part, step, core_ref):
        kind = unit_of(side, step, core_ref) // 2
        return {2: (0, 0), 3: (part, 0, 0), 4: (part, kind, 0, 0)}[right.ndim]

    def send_map(side, part, step, core_ref):
        return (
            jnp.where(side == 0, part, parts - 1),
            jnp.where(side == 0, step, kinds - 1),
            0,
        )

    def keep_map(side, part, step, core_ref):
        return jnp.where(side == 1, part, 0), jnp.where(side == 1, step, 0), 0

    return pl.pallas_call(
        weight_grad_split_kernel,
        grid_spec=pltpu.PrefetchScalarGridSpec(
            num_scalar_prefetch=1,
            grid=(2, parts, kinds),
            in_specs=[
                pl.BlockSpec((1,) * (left.ndim - 2) + (frames, unit), left_map),
                pl.BlockSpec((1,) * (right.ndim - 2) + (frames, columns), right_map),
            ],
            out_specs=[
                pl.BlockSpec((1, unit, columns), send_map),
                pl.BlockSpec((1, unit, columns), keep_map),
            ],
        ),
        out_shape=[shape_of((parts, rows // 2, columns), bf16)] * 2,
        compiler_params=params_of(3),
        cost_estimate=estimate,
        name="weight_grad",
    )(core, left, right)


def add_rounded(*terms):
    total = terms[0].astype(f32)
    for term in terms[1:]:
        total = total + term.astype(f32)
    return total.astype(bf16)


class Relay:
    x01, x10 = [(0, 2), (1, 3)], [(2, 0), (3, 1)]
    y0, y1 = [(0, 1), (1, 0)], [(2, 3), (3, 2)]

    def __init__(self):
        self.section = lax.axis_index("section")
        self.mp = lax.axis_index("mp")
        self.core = lax.axis_index("core")
        self.slot = self.section * 2 + self.mp
        self.parts = 2
        self.core_arg = self.core.astype(jnp.int32).reshape(1)

    def hop(self, values, pairs):
        return lax.ppermute(values, GROUP, pairs)

    def twin(self, values):
        return lax.ppermute(values, "core", [(0, 1), (1, 0)])

    def place(self, layer):
        return jnp.stack([(self.section == layer).astype(jnp.int32), self.core.astype(jnp.int32)])

    def gather(self, weights):
        mine = []
        for weight in weights:
            half = weight.shape[0] // 2
            mine.append(lax.dynamic_slice_in_dim(weight, self.core * half, half, 0))
        first, second = [], []
        for weight, half in zip(weights, mine):
            across = self.hop(half, self.x01)
            beside = self.hop(half, self.y0)
            far = self.hop(across, self.y1)
            first.append((weight, beside, self.twin(beside), across, self.twin(across), far, self.twin(far)))
        for index, (weight, half) in enumerate(zip(weights, mine)):
            across = self.hop(half, self.x10)
            if index < 2:
                beside = self.hop(half, self.y1)
                far = self.hop(beside, self.x10)
            else:
                far = self.hop(across, self.y0)
                beside = self.hop(far, self.x01)
            second.append((weight, beside, self.twin(beside), across, self.twin(across), far, self.twin(far)))
        return first, second

    def order(self, values):
        return jnp.where(self.mp == 0, values, values[::-1])

    unorder = order

    def own_cotangent(self, cotangent):
        shard = cotangent.shape[1]
        rest = LIVE - shard
        to_one = self.hop(cotangent[1], [(0, 1)])
        to_zero = self.hop(cotangent[0, :rest], [(1, 0)])
        to_two = self.hop(cotangent[2, :rest], [(3, 2)])
        natural = [
            jnp.concatenate([cotangent[0], to_zero], 0),
            jnp.concatenate([to_one, cotangent[1, :rest]], 0),
            jnp.concatenate([cotangent[2], to_two], 0),
        ]
        live = jnp.where(self.slot == 0, natural[0], jnp.where(self.slot == 1, natural[1], natural[2]))
        return jnp.where(self.slot < 3, live, jnp.zeros_like(live))

    def to_owners(self, rows, layer, shard):
        head, tail = rows[:shard], rows[shard:]
        pad = lambda v: jnp.concatenate([v, jnp.zeros((shard - v.shape[0], v.shape[1]), v.dtype)], 0)
        outs = []
        for source in range(3):
            got = None
            for mp_index, piece in ((0, head), (1, tail)):
                target = 2 * layer + mp_index
                if target == source:
                    value = jnp.where(self.slot == source, piece, jnp.zeros_like(piece))
                else:
                    value = self.hop(piece, [(source, target)])
                value = value if value.shape[0] == shard else pad(value)
                got = value if got is None else got + value
            outs.append(got)
        return jnp.stack(outs)

    def reduce_near(self, send, keep):
        received = self.twin(send)
        near = add_rounded(keep[0], received[0])
        away = add_rounded(keep[1], received[1])
        return near, self.hop(away, self.y0 + self.y1)

    def reduce_first(self, send, keep):
        total = add_rounded(*self.reduce_near(send, keep))
        return total, self.hop(total, self.x01)

    def reduce_last(self, second, send, keep):
        total = add_rounded(*self.reduce_near(send, keep))
        arrived = self.hop(total, self.x10)
        here = self.section == 0
        own = jnp.where(here, total, second[0])
        other = jnp.where(here, arrived, second[1])
        summed = lax.psum(add_rounded(own, other), "z")
        return lax.all_gather(summed, "core", axis=0, tiled=True).astype(f32)


class General:
    def __init__(self, sections, mps):
        self.sections, self.mps = sections, mps
        self.section = lax.axis_index("section")
        self.mp = lax.axis_index("mp")
        self.slot = self.section * mps + self.mp
        self.parts = mps
        self.core_arg = None

    def place(self, layer):
        return jnp.zeros((2,), jnp.int32)

    def gather(self, weights):
        lists = [[] for _ in range(self.sections)]
        for weight in weights:
            every = lax.all_gather(weight, GROUP, axis=0, tiled=False)
            for layer in range(self.sections):
                lists[layer].append(tuple(every[layer * self.mps + part] for part in range(self.mps)))
        return lists

    def order(self, values):
        return values

    unorder = order

    def own_cotangent(self, cotangent):
        every = lax.all_gather(cotangent, "mp", axis=1, tiled=True)
        count = cotangent.shape[0]
        live = lax.dynamic_index_in_dim(every, jnp.minimum(self.slot, count - 1), 0, False)[:LIVE]
        return jnp.where(self.slot < count, live, jnp.zeros_like(live))

    def to_owners(self, rows, layer, shard):
        every = lax.all_gather(rows, GROUP, axis=0, tiled=False)[:3]
        padded = jnp.pad(every, ((0, 0), (0, shard * self.mps - rows.shape[0]), (0, 0)))
        return lax.dynamic_slice_in_dim(padded, self.mp * shard, shard, 1)

    def reduce_first(self, grads):
        return grads

    def reduce_last(self, second, grads):
        both = lax.psum(jnp.stack([grads, second]), ("section", "mp", "z", "core"))
        mine = lax.dynamic_index_in_dim(both, self.section, 0, False)
        return lax.dynamic_index_in_dim(mine, self.mp, 0, False).astype(f32)


def sinusoid(step_values, table_width):
    half_count = table_width // 2
    log_rate = math.log(10000.0) / (half_count - 1)
    frequency = jnp.exp(jnp.arange(half_count, dtype=f32) * -log_rate)
    angles = step_values.astype(f32)[:, None] * frequency[None, :]
    return jnp.concatenate([jnp.sin(angles), jnp.cos(angles)], 1)


def roll_rows(rows, start):
    return lax.dynamic_slice_in_dim(jnp.concatenate([rows, rows], 0), start, rows.shape[0], 0)


def on_device(
    frame_features,
    clip_lengths,
    audio_drop,
    text_drop,
    timesteps,
    cotangent,
    embed_weight,
    embed_bias,
    time_hidden_weight,
    time_hidden_bias,
    time_output_weight,
    time_output_bias,
    modulate_weight,
    modulate_bias,
    project_weight,
    project_bias,
    output_weight,
    output_bias,
    expand_weight,
    expand_bias,
    shrink_weight,
    shrink_bias,
):
    micro_count, frames, channels = frame_features.shape
    clip_count = clip_lengths.shape[2]
    width = cotangent.shape[2]
    shard = cotangent.shape[1]
    sections, mps = lax.axis_size("section"), lax.axis_size("mp")
    replicas = lax.axis_size("z") * lax.axis_size("core")
    group_size = sections * mps
    if sections == 2 and mps == 2 and micro_count == 3:
        net = Relay()
    else:
        net = General(sections, mps)
    parts, section, mp_index = net.parts, net.section, net.mp
    everyone = ("section", "mp", "z", "core")

    head_columns = project_weight.shape[3]
    project_own = jnp.transpose(project_weight[0], (1, 0, 2)).reshape(3 * width, head_columns)
    weights = net.gather((project_own, output_weight[0], expand_weight[0], shrink_weight[0]))

    small = (
        jnp.concatenate([project_bias[0].reshape(-1), expand_bias[0]]),
        jnp.concatenate([output_bias[0], shrink_bias[0]]),
    )
    shared_bias = lax.all_gather(jnp.concatenate(small), GROUP, axis=0, tiled=False).astype(f32)
    shared_bias = shared_bias.reshape(sections, mps, -1)
    split_bias = 3 * head_columns
    hidden_columns = expand_bias.shape[1]
    project_biases, expand_biases, output_biases, shrink_biases = [], [], [], []
    for layer in range(sections):
        one_layer = shared_bias[layer]
        project_biases.append(net.order(one_layer[:, :split_bias].reshape(mps, 3, head_columns)))
        expand_biases.append(
            net.order(one_layer[:, split_bias : split_bias + hidden_columns].reshape(mps, 1, hidden_columns))
        )
        tail = one_layer[0, split_bias + hidden_columns :]
        output_biases.append(tail[:width][None])
        shrink_biases.append(tail[width:][None])
    embed_full = lax.all_gather(
        jnp.concatenate([embed_weight, embed_bias[None]], 0), "mp", axis=1, tiled=True
    )
    embed_matrix, embed_offset = embed_full[:channels], embed_full[channels:].astype(f32)

    own_clips = micro_count * clip_count
    every_step = lax.all_gather(timesteps.reshape(-1), ("z", "core"), axis=0, tiled=True)
    table = sinusoid(every_step, time_hidden_weight.shape[0])
    hidden_pre = dot_split(table, time_hidden_weight) + time_hidden_bias.astype(f32)
    inner_time, inner_pull = jax.vjp(jax.nn.silu, hidden_pre)
    time_embed = dot_split(inner_time, time_output_weight) + time_output_bias.astype(f32)
    activated, silu_pull = jax.vjp(jax.nn.silu, time_embed)
    replica = lax.axis_index("z") * lax.axis_size("core") + lax.axis_index("core")
    activated_own = lax.dynamic_slice_in_dim(activated, replica * own_clips, own_clips, 0)
    modulate = jnp.transpose(modulate_weight[0], (1, 0, 2))
    high, low = split_rows(activated_own)
    both = jnp.einsum(
        "cd,jde->jce", jnp.concatenate([high, low], 0), modulate, preferred_element_type=f32
    )
    modulation = both[:, :own_clips] + both[:, own_clips:] + modulate_bias[0].astype(f32)[:, None]
    modulation = lax.all_gather(modulation, GROUP, axis=0, tiled=False)

    buffer = jnp.minimum(net.slot, micro_count - 1)
    pick = lambda values: lax.dynamic_index_in_dim(values, buffer, 0, False)
    lengths = pick(clip_lengths)[0]
    ends = jnp.cumsum(lengths)
    starts = ends - lengths
    longest = jnp.argmax(lengths)
    first = jnp.sum(jnp.where(jnp.arange(clip_count) == longest, starts, 0))
    frame_index = jnp.arange(LIVE, dtype=jnp.int32)
    frame_index = jnp.where(frame_index + first >= LIVE, frame_index + first - LIVE, frame_index + first)
    member = (frame_index[:, None] >= starts[None]) & (frame_index[:, None] < ends[None])
    onehot = member.astype(f32)
    position = jnp.sum(jnp.where(member, frame_index[:, None] - starts[None], 0), 1).astype(f32)
    segment = jnp.sum(jnp.where(member, jnp.arange(clip_count)[None], 0), 1).astype(f32)
    one = jnp.concatenate([onehot, onehot], 1).astype(bf16)
    seg_row, seg_column = segment[None, LONGEST:], segment[LONGEST:, None]
    lane = jnp.arange(LANES)
    inverse = 1.0 / 10000.0 ** ((lane % HEAD // 2).astype(f32) * 2.0 / HEAD)
    angles = position[:, None] * inverse[None]
    cosine = jnp.cos(angles)
    sine = jnp.sin(angles) * jnp.where(lane % 2 == 0, -1.0, 1.0)[None]

    columns = jnp.arange(channels)
    audio_columns = ((columns >= MEL) & (columns < 2 * MEL)).astype(f32)
    text_columns = (columns >= 2 * MEL).astype(f32)
    audio_keep = jnp.sum(onehot * (1 - pick(audio_drop)).astype(f32), 1)
    text_keep = jnp.sum(onehot * (1 - pick(text_drop)).astype(f32), 1)
    factor = (
        (1.0 - audio_columns - text_columns)[None]
        + audio_keep[:, None] * audio_columns[None]
        + text_keep[:, None] * text_columns[None]
    )
    masked = roll_rows(pick(frame_features)[:LIVE], first) * factor.astype(bf16)
    entry = (dot_nn(masked, embed_matrix) + embed_offset).astype(bf16)

    modulation = modulation.reshape(sections, mps, 6, micro_count, clip_count, -1)
    modulation = lax.dynamic_index_in_dim(modulation, buffer, 3, False)
    modulation = jnp.transpose(modulation, (0, 3, 2, 1, 4)).reshape(sections, clip_count, 6 * width)
    mod_high, mod_low = split_rows(modulation)
    mods = jnp.concatenate([mod_high, mod_low], 1)

    cot_rows = roll_rows(net.own_cotangent(cotangent), first)

    stream, kept, outputs = entry, [], []
    for layer in range(2):
        place, mod = net.place(layer), mods[layer]
        project_refs, out_refs, in_refs, shrink_refs = weights[layer]
        normed_a, heads = project(
            place, stream, one, mod[:, : 2 * width], project_biases[layer], cosine, sine,
            project_refs, parts, head_columns,
        )
        attended, totals = attend(seg_row, seg_column, heads)
        mid, branch_a, normed_f, inner, branch_f, stream_out = feed(
            place, stream, attended, one, mod[:, 2 * width :],
            output_biases[layer], expand_biases[layer], shrink_biases[layer],
            out_refs, in_refs, shrink_refs,
        )
        kept.append((stream, normed_a, heads, attended, totals, mid, branch_a, normed_f, inner, branch_f))
        outputs.append(roll_rows(stream_out, LIVE - first))
        stream = stream_out

    grad, gradients, second = cot_rows, [None, None], None
    clip_sums, row_totals, inner_totals, head_totals = [None, None], [None, None], [None, None], [None, None]
    reduced = []
    for layer in (1, 0):
        place, mod = net.place(layer), mods[layer]
        project_refs, out_refs, in_refs, shrink_refs = weights[layer]
        x, normed_a, heads, attended, totals, mid, branch_a, normed_f, inner, branch_f = kept[layer]
        gf, hidden, dinner, ga, datt, gmid, dmod_f, row_sums, inner_sums = feed_back(
            place, grad, inner, mid, branch_a, branch_f, one, mod[:, 2 * width :],
            out_refs, in_refs, shrink_refs, head_columns,
        )
        partials = [None] * 4
        partials[3] = weight_grad(net.core_arg, hidden, gf, parts)
        partials[2] = weight_grad(net.core_arg, normed_f, dinner, parts)
        partials[1] = weight_grad(net.core_arg, attended, ga, parts)
        dheads = attend_back(seg_row, seg_column, cosine, sine, heads, attended, datt, totals)
        partials[0] = weight_grad(net.core_arg, normed_a, dheads, parts)
        grad, dmod_a, head_sums = project_back(
            place, gmid, x, dheads, one, mod[:, width : 2 * width], project_refs
        )
        gradients[layer] = roll_rows(grad, LIVE - first)
        clip_sums[layer] = jnp.concatenate([dmod_a, dmod_f], 0)[:, :clip_count]
        row_totals[layer] = jnp.sum(row_sums[:, :clip_count], 1)
        inner_totals[layer] = net.unorder(jnp.sum(inner_sums[:, :clip_count], 1))
        head_totals[layer] = net.unorder(jnp.sum(head_sums[:, :, :clip_count], 2))
        if layer == 1:
            second = [net.reduce_first(*(p if isinstance(p, (list, tuple)) else (p,))) for p in partials]
        else:
            reduced = [
                net.reduce_last(s, *(p if isinstance(p, (list, tuple)) else (p,)))
                for s, p in zip(second, partials)
            ]

    row_start = mp_index * shard
    shard_rows = row_start + jnp.arange(shard, dtype=jnp.int32)
    padding = (shard_rows >= LIVE)[None, :, None]
    shard_mel = lax.dynamic_slice_in_dim(frame_features, row_start, shard, 1)[:, :, :MEL]
    pad_entry = (
        jnp.einsum("mfe,ed->mfd", shard_mel, embed_matrix[:MEL], preferred_element_type=f32)
        + embed_offset
    ).astype(bf16)
    streams = [net.to_owners(outputs[layer], layer, shard) for layer in range(2)]
    stream_grads = [net.to_owners(gradients[layer], layer, shard) for layer in range(2)]
    here = section == 0
    stream_all = jnp.where(padding, pad_entry, jnp.where(here, streams[0], streams[1]))[None]
    grad_all = jnp.where(padding, cotangent, jnp.where(here, stream_grads[0], stream_grads[1]))
    grad_all = grad_all.astype(f32)[None]

    pad_grad = jnp.where(padding & here, cotangent, jnp.zeros_like(cotangent))
    embed_partial = dot_tn(masked, grad)
    mel_partial = jnp.einsum("mfe,mfd->ed", shard_mel, pad_grad, preferred_element_type=f32)
    embed_partial = jnp.concatenate([embed_partial[:MEL] + mel_partial, embed_partial[MEL:]], 0)
    embed_sum = jnp.sum(grad.astype(f32), 0) + jnp.sum(pad_grad.astype(f32), (0, 1))
    embed_near = lax.psum_scatter(
        embed_partial.astype(bf16), "mp", scatter_dimension=1, tiled=True
    )
    embed_weight_grad = lax.psum(embed_near, ("section", "z", "core")).astype(f32)

    pieces = [embed_sum]
    for layer in range(2):
        pieces += [
            row_totals[layer].reshape(-1),
            inner_totals[layer].reshape(-1),
            head_totals[layer].reshape(-1),
        ]
    vector = lax.psum(jnp.concatenate(pieces), everyone)
    embed_bias_grad = lax.dynamic_slice_in_dim(vector[:width], mp_index * (width // mps), width // mps, 0)
    per_layer = vector[width:].reshape(2, -1)
    layer_vector = jnp.where(here, per_layer[0], per_layer[1])
    shrink_bias_grad = layer_vector[:width]
    output_bias_grad = layer_vector[width : 2 * width]
    inner_end = 2 * width + mps * hidden_columns
    expand_bias_grad = lax.dynamic_index_in_dim(
        layer_vector[2 * width : inner_end].reshape(mps, -1), mp_index, 0, False
    )
    project_bias_grad = lax.dynamic_index_in_dim(
        layer_vector[inner_end:].reshape(mps, 3, -1), mp_index, 0, False
    )

    clip_all = jnp.stack(clip_sums)
    clip_all = lax.all_gather(clip_all, GROUP, axis=0, tiled=False)[:micro_count]
    clip_own = lax.dynamic_index_in_dim(clip_all, section, 1, False)
    clip_own = lax.dynamic_slice_in_dim(clip_own, mp_index * (width // mps), width // mps, 3)
    clip_own = jnp.transpose(clip_own, (1, 0, 2, 3)).reshape(6, own_clips, -1)
    clip_every = lax.all_gather(clip_own, ("z", "core"), axis=1, tiled=True)
    modulate_bias_grad = jnp.sum(clip_every, 1)
    clip_low = clip_every.astype(bf16)
    modulate_weight_grad = jnp.einsum(
        "cd,jce->jde", activated.astype(bf16), clip_low, preferred_element_type=f32
    )
    activated_part = jnp.einsum("jce,jde->cd", clip_low, modulate, preferred_element_type=f32)
    activated_grad = lax.psum(activated_part, GROUP)
    time_grad = silu_pull(activated_grad)[0]
    time_low = time_grad.astype(bf16)
    time_output_grad = dot_tn(inner_time.astype(bf16), time_low)
    hidden_grad = inner_pull(dot_nt(time_low, time_output_weight))[0]
    time_hidden_grad = dot_tn(table.astype(bf16), hidden_grad.astype(bf16))

    project_grad = jnp.transpose(reduced[0].reshape(3, width, head_columns), (1, 0, 2))
    return (
        stream_all,
        grad_all,
        embed_weight_grad,
        embed_bias_grad,
        time_hidden_grad,
        jnp.sum(hidden_grad, 0),
        time_output_grad,
        jnp.sum(time_grad, 0),
        jnp.transpose(modulate_weight_grad, (1, 0, 2))[None],
        modulate_bias_grad[None],
        project_grad[None],
        project_bias_grad[None],
        reduced[1][None],
        output_bias_grad[None],
        reduced[2][None],
        expand_bias_grad[None],
        reduced[3][None],
        shrink_bias_grad[None],
    )


def solution(mesh):
    sections, replicas, mps = (mesh.shape[name] for name in ("section", "dp", "mp"))
    fine = Mesh(mesh.devices.reshape(sections, replicas // 2, 2, mps), ("section", "z", "core", "mp"))
    dp = ("z", "core")
    return jax.shard_map(
        on_device,
        mesh=fine,
        in_specs=(
            P(None, dp, None),
            P(None, dp, None),
            P(None, dp, None),
            P(None, dp, None),
            P(None, dp, None),
            P(None, ("z", "core", "mp"), None),
            P(None, "mp"),
            P("mp"),
            P(),
            P(),
            P(),
            P(),
            P("section", None, None, "mp"),
            P("section", None, "mp"),
            P("section", None, None, "mp"),
            P("section", None, "mp"),
            P("section", "mp", None),
            P("section", None),
            P("section", None, "mp"),
            P("section", "mp"),
            P("section", "mp", None),
            P("section", None),
        ),
        out_specs=(
            P("section", None, ("z", "core", "mp"), None),
            P("section", None, ("z", "core", "mp"), None),
            P(None, "mp"),
            P("mp"),
            P(),
            P(),
            P(),
            P(),
            P("section", None, None, "mp"),
            P("section", None, "mp"),
            P("section", None, None, "mp"),
            P("section", None, "mp"),
            P("section", "mp", None),
            P("section", None),
            P("section", None, "mp"),
            P("section", "mp"),
            P("section", "mp", None),
            P("section", None),
        ),
        check_vma=False,
    )
```

```python
import math

import jax
import jax.numpy as jnp
from jax import lax
from jax.experimental import pallas as pl
from jax.experimental.pallas import tpu as pltpu
from jax.sharding import Mesh
from jax.sharding import PartitionSpec as P

HEAD = 64
MEL = 100
LIVE = 768
LONGEST = 512
BLOCK = 256
LANES = 128
EPS = 1e-06
MASKED = -1e30
SCORE = math.log2(math.e) / math.sqrt(HEAD)
GELU = math.sqrt(2.0 / math.pi)

f32 = jnp.float32
bf16 = jnp.bfloat16
GROUP = ("section", "mp")
VMEM_LIMIT = 56 << 20


def dot_of(left, right, left_dim, right_dim):
    return lax.dot_general(
        left, right, (((left_dim,), (right_dim,)), ((), ())), preferred_element_type=f32
    )


def dot_nn(left, right):
    return dot_of(left, right, 1, 0)


def dot_nt(left, right):
    return dot_of(left, right, 1, 1)


def dot_tn(left, right):
    return dot_of(left, right, 0, 0)


def split_rows(values):
    high = values.astype(bf16)
    low = (values - high.astype(f32)).astype(bf16)
    return high, low


def dot_split(left, right):
    high, low = split_rows(left)
    both = dot_nn(jnp.concatenate([high, low], 0), right)
    rows = left.shape[0]
    return both[:rows] + both[rows:]


def whole_spec(value):
    rank = len(value.shape)
    return pl.BlockSpec(value.shape, lambda *_: (0,) * rank)


def any_spec():
    return pl.BlockSpec(memory_space=pl.ANY)


def smem_spec():
    return pl.BlockSpec(memory_space=pltpu.SMEM)


def shape_of(shape, kind):
    return jax.ShapeDtypeStruct(shape, kind)


def params_of(axes):
    return pltpu.CompilerParams(
        dimension_semantics=("arbitrary",) * axes, vmem_limit_bytes=VMEM_LIMIT
    )


def cost(flops, moved, special=0):
    return pl.CostEstimate(flops=int(flops), bytes_accessed=int(moved), transcendentals=int(special))


def start_fetch(place, refs, store, sems):
    parts, rows = store.shape[0], store.shape[1]
    if len(refs) == parts:
        for part in range(parts):
            pltpu.make_async_copy(refs[part], store.at[part], sems.at[part]).start()
        return
    own, mp_mine, mp_twin, sec_mine, sec_twin, far_mine, far_twin = refs
    half = rows // 2
    mine = pl.ds(pl.multiple_of(place[1] * half, half), half)
    twin = pl.ds(pl.multiple_of((1 - place[1]) * half, half), half)

    def halves(part, first, second):
        pltpu.make_async_copy(first, store.at[part, mine], sems.at[part]).start()
        pltpu.make_async_copy(second, store.at[part, twin], sems.at[part]).start()

    @pl.when(place[0] == 1)
    def _here():
        pltpu.make_async_copy(own, store.at[0], sems.at[0]).start()
        halves(1, mp_mine, mp_twin)

    @pl.when(place[0] != 1)
    def _there():
        halves(0, sec_mine, sec_twin)
        halves(1, far_mine, far_twin)


def wait_fetch(store, sems, part):
    pltpu.make_async_copy(store.at[part], store.at[part], sems.at[part]).wait()


def store_of(parts, rows, columns):
    return [pltpu.VMEM((parts, rows, columns), bf16), pltpu.SemaphoreType.DMA((parts,))]


def normal(rows):
    centered = rows - jnp.mean(rows, -1, keepdims=True)
    inverse = lax.rsqrt(jnp.mean(centered * centered, -1, keepdims=True) + EPS)
    return centered * inverse, inverse


def normal_back(unit, inverse, grad):
    return inverse * (
        grad
        - jnp.mean(grad, -1, keepdims=True)
        - unit * jnp.mean(grad * unit, -1, keepdims=True)
    )


def turn(values, cosine, sine):
    lane = lax.broadcasted_iota(jnp.int32, (values.shape[0], LANES), 1)
    even = lane % 2 == 0
    pieces = []
    for start in range(0, values.shape[1], LANES):
        piece = values[:, start : start + LANES]
        other = jnp.where(even, pltpu.roll(piece, LANES - 1, 1), pltpu.roll(piece, 1, 1))
        pieces.append(piece * cosine + other * sine)
    return pieces[0] if len(pieces) == 1 else jnp.concatenate(pieces, 1)


def gelu_parts(inner):
    square = inner * inner
    bend = jnp.tanh(GELU * inner * (1.0 + 0.044715 * square))
    half = 0.5 * (1.0 + bend)
    slope = half + 0.5 * inner * (1.0 - bend * bend) * (GELU * (1.0 + 0.134145 * square))
    return inner * half, slope


def project_kernel(place, x, one, mod, bias, cosine, sine, *rest):
    (normed, heads), (store, sems) = rest[-4:-2], rest[-2:]
    refs = rest[:-4]
    width = x.shape[1]
    columns = store.shape[2]
    step = pl.program_id(0)

    @pl.when(step == 0)
    def _start():
        start_fetch(place, refs, store, sems)

    shift_scale = dot_nn(one[...], mod[...])
    unit, _ = normal(x[...].astype(f32))
    rows = (unit * (1.0 + shift_scale[:, width:]) + shift_scale[:, :width]).astype(bf16)
    normed[...] = rows
    for part in range(store.shape[0]):

        @pl.when(step == 0)
        def _wait(part=part):
            wait_fetch(store, sems, part)

        for kind in range(3):
            out = dot_nn(rows, store[part, kind * width : (kind + 1) * width, :])
            out = out + bias[part, kind : kind + 1, :]
            if kind < 2:
                out = turn(out, cosine[...], sine[...])
            heads[part, kind] = out.astype(bf16)


def project(place, x, one, mod, bias, cosine, sine, refs, parts, columns):
    rows, width = x.shape
    row_block = lambda w: pl.BlockSpec((BLOCK, w), lambda i: (i, 0))
    return pl.pallas_call(
        project_kernel,
        grid=(rows // BLOCK,),
        in_specs=[
            smem_spec(),
            row_block(width),
            row_block(one.shape[1]),
            whole_spec(mod),
            whole_spec(bias),
            row_block(LANES),
            row_block(LANES),
        ]
        + [any_spec()] * len(refs),
        out_specs=[
            row_block(width),
            pl.BlockSpec((parts, 3, BLOCK, columns), lambda i: (0, 0, i, 0)),
        ],
        out_shape=[
            shape_of((rows, width), bf16),
            shape_of((parts, 3, rows, columns), bf16),
        ],
        scratch_shapes=store_of(parts, 3 * width, columns),
        compiler_params=params_of(1),
        cost_estimate=cost(6 * rows * width * columns * parts, 14 << 20),
        name="project",
    )(place, x, one, mod, bias, cosine, sine, *refs)


def attend_block(key, query, value, allowed):
    lane = lax.broadcasted_iota(jnp.int32, key.shape, 1)
    value_t = value.astype(f32).T.astype(bf16)
    outs, totals = [], []
    for head in range(2):
        mine = (lane < HEAD) if head == 0 else (lane >= HEAD)
        scores = dot_nt(jnp.where(mine, key, jnp.zeros_like(key)), query)
        if allowed is not None:
            scores = jnp.where(allowed, scores, MASKED)
        top = jnp.max(scores, 0, keepdims=True)
        weights = jnp.exp2((scores - top) * SCORE)
        total = jnp.sum(weights, 0, keepdims=True)
        out = dot_nn(value_t[head * HEAD : (head + 1) * HEAD], weights.astype(bf16))
        outs.append(out / total)
        totals.append(top * SCORE + jnp.log2(total))
    return jnp.concatenate(outs, 0).T, jnp.concatenate(totals, 0)


def attend_kernel(seg_row, seg_column, heads, attended, totals):
    allowed = seg_column[...] == seg_row[...]
    for rows, mask in ((pl.ds(0, LONGEST), None), (pl.ds(LONGEST, LIVE - LONGEST), allowed)):
        out, total = attend_block(heads[0, 1, rows], heads[0, 0, rows], heads[0, 2, rows], mask)
        attended[0, rows, :] = out.astype(bf16)
        totals[0, 0, :, rows] = total


def attend(seg_row, seg_column, heads):
    parts, _, rows, columns = heads.shape
    pairs = columns // LANES
    return pl.pallas_call(
        attend_kernel,
        grid=(parts, pairs),
        in_specs=[
            whole_spec(seg_row),
            whole_spec(seg_column),
            pl.BlockSpec((1, 3, rows, LANES), lambda i, j: (i, 0, 0, j)),
        ],
        out_specs=[
            pl.BlockSpec((1, rows, LANES), lambda i, j: (i, 0, j)),
            pl.BlockSpec((1, 1, 2, rows), lambda i, j: (i, j, 0, 0)),
        ],
        out_shape=[
            shape_of((parts, rows, columns), bf16),
            shape_of((parts, pairs, 2, rows), f32),
        ],
        compiler_params=params_of(2),
        cost_estimate=cost(8 << 30, 8 << 20),
        name="attend",
    )(seg_row, seg_column, heads)


def feed_kernel(place, x, attended, one, mod, out_bias, in_bias, shrink_bias, *rest):
    stores = rest[-6:]
    mid, branch_a, normed, inner, branch_f, x_out = rest[-12:-6]
    refs = rest[:-12]
    third = len(refs) // 3
    out_store, out_sems, in_store, in_sems, shrink_store, shrink_sems = stores
    parts = out_store.shape[0]
    width = x.shape[1]
    step = pl.program_id(0)

    @pl.when(step == 0)
    def _start():
        start_fetch(place, refs[:third], out_store, out_sems)
        start_fetch(place, refs[third : 2 * third], in_store, in_sems)
        start_fetch(place, refs[2 * third :], shrink_store, shrink_sems)

    def arrive(store, sems, part):
        @pl.when(step == 0)
        def _wait():
            wait_fetch(store, sems, part)

    token = dot_nn(one[...], mod[...])
    branch = out_bias[...]
    for part in range(parts):
        arrive(out_store, out_sems, part)
        branch = branch + dot_nn(attended[part], out_store[part])
    branch_a[...] = branch.astype(bf16)
    middle = x[...].astype(f32) + token[:, :width] * branch
    mid[...] = middle
    unit, _ = normal(middle)
    rows = (unit * (1.0 + token[:, 2 * width : 3 * width]) + token[:, width : 2 * width]).astype(bf16)
    normed[...] = rows
    hidden = []
    for part in range(parts):
        arrive(in_store, in_sems, part)
        act = dot_nn(rows, in_store[part]) + in_bias[part]
        inner[part] = act.astype(bf16)
        bend = jnp.tanh(GELU * act * (1.0 + 0.044715 * act * act))
        hidden.append((act * (0.5 + 0.5 * bend)).astype(bf16))
    branch = shrink_bias[...]
    for part in range(parts):
        arrive(shrink_store, shrink_sems, part)
        branch = branch + dot_nn(hidden[part], shrink_store[part])
    branch_f[...] = branch.astype(bf16)
    x_out[...] = (middle + token[:, 3 * width :] * branch).astype(bf16)


def feed(place, x, attended, one, mod, out_bias, in_bias, shrink_bias, out_refs, in_refs, shrink_refs):
    rows, width = x.shape
    parts, _, columns = attended.shape
    hidden = in_bias.shape[2]
    row_block = lambda w: pl.BlockSpec((BLOCK, w), lambda i: (i, 0))
    part_block = lambda w: pl.BlockSpec((parts, BLOCK, w), lambda i: (0, i, 0))
    return pl.pallas_call(
        feed_kernel,
        grid=(rows // BLOCK,),
        in_specs=[
            smem_spec(),
            row_block(width),
            part_block(columns),
            row_block(one.shape[1]),
            whole_spec(mod),
            whole_spec(out_bias),
            whole_spec(in_bias),
            whole_spec(shrink_bias),
        ]
        + [any_spec()] * (3 * len(out_refs)),
        out_specs=[
            row_block(width),
            row_block(width),
            row_block(width),
            part_block(hidden),
            row_block(width),
            row_block(width),
        ],
        out_shape=[
            shape_of((rows, width), f32),
            shape_of((rows, width), bf16),
            shape_of((rows, width), bf16),
            shape_of((parts, rows, hidden), bf16),
            shape_of((rows, width), bf16),
            shape_of((rows, width), bf16),
        ],
        scratch_shapes=store_of(parts, columns, width)
        + store_of(parts, width, hidden)
        + store_of(parts, hidden, width),
        compiler_params=params_of(1),
        cost_estimate=cost(2 * rows * width * parts * (columns + 2 * hidden), 24 << 20),
        name="feed",
    )(place, x, attended, one, mod, out_bias, in_bias, shrink_bias, *out_refs, *in_refs, *shrink_refs)


def feed_back_kernel(place, grad, inner, mid, branch_a, branch_f, one, mod, *rest):
    stores = rest[-6:]
    outs = rest[-15:-6]
    refs = rest[:-15]
    gf_out, hidden_out, dinner_out, ga_out, datt_out, gmid_out, dmod, row_sums, inner_sums = outs
    third = len(refs) // 3
    out_store, out_sems, in_store, in_sems, shrink_store, shrink_sems = stores
    parts = out_store.shape[0]
    width = grad.shape[1]
    step = pl.program_id(0)

    @pl.when(step == 0)
    def _start():
        start_fetch(place, refs[2 * third :], shrink_store, shrink_sems)
        start_fetch(place, refs[third : 2 * third], in_store, in_sems)
        start_fetch(place, refs[:third], out_store, out_sems)
        dmod[...] = jnp.zeros_like(dmod)
        row_sums[...] = jnp.zeros_like(row_sums)
        inner_sums[...] = jnp.zeros_like(inner_sums)

    def arrive(store, sems, part):
        @pl.when(step == 0)
        def _wait():
            wait_fetch(store, sems, part)

    token = dot_nn(one[...], mod[...])
    member = one[...]
    g = grad[...].astype(f32)
    gf = (token[:, 3 * width :] * g).astype(bf16)
    gf_out[...] = gf
    row_sums[0] += dot_tn(member, gf)
    dmod[3] += dot_tn(member, (g * branch_f[...].astype(f32)).astype(bf16))
    dnormed = None
    for part in range(parts):
        arrive(shrink_store, shrink_sems, part)
        dhidden = dot_nt(gf, shrink_store[part])
        value, slope = gelu_parts(inner[part].astype(f32))
        hidden_out[part] = value.astype(bf16)
        dinner = (slope * dhidden).astype(bf16)
        dinner_out[part] = dinner
        inner_sums[part] += dot_tn(member, dinner)
        arrive(in_store, in_sems, part)
        piece = dot_nt(dinner, in_store[part])
        dnormed = piece if dnormed is None else dnormed + piece
    unit, inverse = normal(mid[...])
    dmod[1] += dot_tn(member, dnormed.astype(bf16))
    dmod[2] += dot_tn(member, (dnormed * unit).astype(bf16))
    gmid = g + normal_back(unit, inverse, dnormed * (1.0 + token[:, 2 * width : 3 * width]))
    gmid_out[...] = gmid
    dmod[0] += dot_tn(member, (gmid * branch_a[...].astype(f32)).astype(bf16))
    ga = (token[:, :width] * gmid).astype(bf16)
    ga_out[...] = ga
    row_sums[1] += dot_tn(member, ga)
    for part in range(parts):
        arrive(out_store, out_sems, part)
        datt_out[part] = dot_nt(ga, out_store[part]).astype(bf16)


def feed_back(place, grad, inner, mid, branch_a, branch_f, one, mod, out_refs, in_refs, shrink_refs, columns):
    rows, width = grad.shape
    parts, _, hidden = inner.shape
    row_block = lambda w: pl.BlockSpec((BLOCK, w), lambda i: (i, 0))
    part_block = lambda w: pl.BlockSpec((parts, BLOCK, w), lambda i: (0, i, 0))
    clips = one.shape[1]
    fixed = lambda *shape: pl.BlockSpec(shape, lambda i: (0,) * len(shape))
    return pl.pallas_call(
        feed_back_kernel,
        grid=(rows // BLOCK,),
        in_specs=[
            smem_spec(),
            row_block(width),
            part_block(hidden),
            row_block(width),
            row_block(width),
            row_block(width),
            row_block(clips),
            whole_spec(mod),
        ]
        + [any_spec()] * (3 * len(out_refs)),
        out_specs=[
            row_block(width),
            part_block(hidden),
            part_block(hidden),
            row_block(width),
            part_block(columns),
            row_block(width),
            fixed(4, clips, width),
            fixed(2, clips, width),
            fixed(parts, clips, hidden),
        ],
        out_shape=[
            shape_of((rows, width), bf16),
            shape_of((parts, rows, hidden), bf16),
            shape_of((parts, rows, hidden), bf16),
            shape_of((rows, width), bf16),
            shape_of((parts, rows, columns), bf16),
            shape_of((rows, width), f32),
            shape_of((4, clips, width), f32),
            shape_of((2, clips, width), f32),
            shape_of((parts, clips, hidden), f32),
        ],
        scratch_shapes=store_of(parts, columns, width)
        + store_of(parts, width, hidden)
        + store_of(parts, hidden, width),
        compiler_params=params_of(1),
        cost_estimate=cost(2 * rows * width * parts * (columns + 2 * hidden), 32 << 20),
        name="feed_back",
    )(place, grad, inner, mid, branch_a, branch_f, one, mod, *out_refs, *in_refs, *shrink_refs)


def attend_back_block(key, query, value, out, dout, totals, allowed):
    lane = lax.broadcasted_iota(jnp.int32, key.shape, 1)
    out_t = out.astype(f32).T
    dout_t = dout.astype(f32).T
    key_t = key.astype(f32).T.astype(bf16)
    centres = out_t * dout_t
    dqueries, dkey, dvalue = [], None, None
    for head in range(2):
        mine = (lane < HEAD) if head == 0 else (lane >= HEAD)
        own = lambda array: jnp.where(mine, array, jnp.zeros_like(array))
        rows = slice(head * HEAD, (head + 1) * HEAD)
        scores = dot_nt(own(key), query)
        if allowed is not None:
            scores = jnp.where(allowed, scores, MASKED)
        weights = jnp.exp2(scores * SCORE - totals[head : head + 1])
        dweights = dot_nt(own(value), dout)
        centre = jnp.sum(centres[rows], 0, keepdims=True)
        dscores = (weights * (dweights - centre)).astype(bf16)
        piece = dot_nn(weights.astype(bf16), own(dout))
        dvalue = piece if dvalue is None else dvalue + piece
        piece = dot_nn(dscores, own(query))
        dkey = piece if dkey is None else dkey + piece
        dqueries.append(dot_nn(key_t[rows], dscores))
    scale = HEAD ** (-0.5)
    return jnp.concatenate(dqueries, 0).T * scale, dkey * scale, dvalue


def attend_back_kernel(seg_row, seg_column, cosine, sine, heads, attended, datt, totals, dheads):
    allowed = seg_column[...] == seg_row[...]
    for rows, mask in ((pl.ds(0, LONGEST), None), (pl.ds(LONGEST, LIVE - LONGEST), allowed)):
        dquery, dkey, dvalue = attend_back_block(
            heads[0, 1, rows],
            heads[0, 0, rows],
            heads[0, 2, rows],
            attended[0, rows],
            datt[0, rows],
            totals[0, 0, :, rows],
            mask,
        )
        dheads[0, 0, rows] = turn(dquery, cosine[rows], -sine[rows]).astype(bf16)
        dheads[0, 1, rows] = turn(dkey, cosine[rows], -sine[rows]).astype(bf16)
        dheads[0, 2, rows] = dvalue.astype(bf16)


def attend_back(seg_row, seg_column, cosine, sine, heads, attended, datt, totals):
    parts, _, rows, columns = heads.shape
    pairs = columns // LANES
    triple = pl.BlockSpec((1, 3, rows, LANES), lambda i, j: (i, 0, 0, j))
    single = pl.BlockSpec((1, rows, LANES), lambda i, j: (i, 0, j))
    return pl.pallas_call(
        attend_back_kernel,
        grid=(parts, pairs),
        in_specs=[
            whole_spec(seg_row),
            whole_spec(seg_column),
            whole_spec(cosine),
            whole_spec(sine),
            triple,
            single,
            single,
            pl.BlockSpec((1, 1, 2, rows), lambda i, j: (i, j, 0, 0)),
        ],
        out_specs=triple,
        out_shape=shape_of(heads.shape, bf16),
        compiler_params=params_of(2),
        cost_estimate=cost(16 << 30, 16 << 20),
        name="attend_back",
    )(seg_row, seg_column, cosine, sine, heads, attended, datt, totals)


def project_back_kernel(place, gmid, x, dheads, one, mod, *rest):
    store, sems = rest[-2:]
    gin, dmod, head_sums = rest[-5:-2]
    refs = rest[:-5]
    width = x.shape[1]
    step = pl.program_id(0)

    @pl.when(step == 0)
    def _start():
        start_fetch(place, refs, store, sems)
        dmod[...] = jnp.zeros_like(dmod)
        head_sums[...] = jnp.zeros_like(head_sums)

    member = one[...]
    dnormed = None
    for part in range(store.shape[0]):

        @pl.when(step == 0)
        def _wait(part=part):
            wait_fetch(store, sems, part)

        for kind in range(3):
            rows = dheads[part, kind]
            head_sums[part, kind] += dot_tn(member, rows)
            piece = dot_nt(rows, store[part, kind * width : (kind + 1) * width, :])
            dnormed = piece if dnormed is None else dnormed + piece
    scale = dot_nn(member, mod[...])
    unit, inverse = normal(x[...].astype(f32))
    dmod[0] += dot_tn(member, dnormed.astype(bf16))
    dmod[1] += dot_tn(member, (dnormed * unit).astype(bf16))
    gin[...] = (gmid[...] + normal_back(unit, inverse, dnormed * (1.0 + scale))).astype(bf16)


def project_back(place, gmid, x, dheads, one, mod, refs):
    rows, width = x.shape
    parts, _, _, columns = dheads.shape
    row_block = lambda w: pl.BlockSpec((BLOCK, w), lambda i: (i, 0))
    clips = one.shape[1]
    fixed = lambda *shape: pl.BlockSpec(shape, lambda i: (0,) * len(shape))
    return pl.pallas_call(
        project_back_kernel,
        grid=(rows // BLOCK,),
        in_specs=[
            smem_spec(),
            row_block(width),
            row_block(width),
            pl.BlockSpec((parts, 3, BLOCK, columns), lambda i: (0, 0, i, 0)),
            row_block(clips),
            whole_spec(mod),
        ]
        + [any_spec()] * len(refs),
        out_specs=[row_block(width), fixed(2, clips, width), fixed(parts, 3, clips, columns)],
        out_shape=[
            shape_of((rows, width), bf16),
            shape_of((2, clips, width), f32),
            shape_of((parts, 3, clips, columns), f32),
        ],
        scratch_shapes=store_of(parts, 3 * width, columns),
        compiler_params=params_of(1),
        cost_estimate=cost(6 * rows * width * columns * parts, 18 << 20),
        name="project_back",
    )(place, gmid, x, dheads, one, mod, *refs)


CHUNKS = 8


def chunk_of(index, core):
    if index < 3:
        return 0, index * 1024 + core * 512, 512
    if index == 3:
        return 1, core * 256, 256
    weight = 2 + (index - 4) // 2
    return weight, core * 512 + 256 * ((index - 4) % 2), 256


class Ring:
    def __init__(self, own, full, link_send, link_recv, twin_send, twin_recv):
        self.own, self.full = own, full
        self.link_send, self.link_recv = link_send, link_recv
        self.twin_send, self.twin_recv = twin_send, twin_recv
        self.x, self.y, self.c = (lax.axis_index(name) for name in ("section", "mp", "core"))
        self.peers = {"x": {"section": 1 - self.x}, "y": {"mp": 1 - self.y}, "twin": {"core": 1 - self.c}}
        self.sent, self.handed = [], []

    def slot(self, index, quarter, core):
        weight, start, rows = chunk_of(index, core)
        start = pl.multiple_of(start, 256)
        return self.full[weight].at[quarter[0], quarter[1], pl.ds(start, rows)]

    def link(self, index, quarter, kind, peer):
        ref = source = self.slot(index, quarter, self.c)
        if kind < 2:
            weight, start, rows = chunk_of(index, self.c)
            source = self.own[weight].at[pl.ds(pl.multiple_of(start, 256), rows)]
        return pltpu.make_async_remote_copy(
            source,
            ref,
            self.link_send.at[index, kind],
            self.link_recv.at[index, quarter[0], quarter[1]],
            device_id=self.peers[peer],
            device_id_type=pl.DeviceIdType.MESH,
        )

    def send(self, index, quarter, kind, peer):
        self.link(index, quarter, kind, peer).start()

    def sent_all(self, kinds):
        for index, quarter, kind, peer in kinds:
            self.link(index, quarter, kind, peer).wait_send()

    def hand(self, index, quarter, core):
        ref = self.slot(index, quarter, core)
        return pltpu.make_async_remote_copy(
            ref,
            ref,
            self.twin_send.at[index, quarter[0], quarter[1]],
            self.twin_recv.at[index, quarter[0], quarter[1]],
            device_id=self.peers["twin"],
            device_id_type=pl.DeviceIdType.MESH,
        )

    def arrive(self, index, quarter):
        self.link(index, quarter, 2, "x").wait_recv()
        self.hand(index, quarter, self.c).start()

    def complete(self, index, quarter):
        self.hand(index, quarter, 1 - self.c).wait_recv()


def barrier(peers):
    semaphore = pltpu.get_barrier_semaphore()
    for peer in peers:
        pl.semaphore_signal(semaphore, inc=1, device_id=peer, device_id_type=pl.DeviceIdType.MESH)
    pl.semaphore_wait(semaphore, len(peers))


def block_rows(index):
    return pl.ds(pl.multiple_of(index * BLOCK, BLOCK), BLOCK)


def forward_kernel(
    own_p, own_o, own_e, own_s, entry, one, mods, p_bias, e_bias, o_bias, s_bias, cosine, sine, seg_row, seg_column,
    full_p, full_o, full_e, full_s, normed_a, heads, attended, totals, mid, branch_a, normed_f, inner, branch_f, x_out,
    v_p, v_o, v_e, v_s, v_x, v_normed, v_heads, v_att, v_tot, v_mid, v_ba, v_nf, v_inner, v_bf,
    link_send, link_recv, twin_send, twin_recv, own_sem, load_sem, x_sem, save_sem,
):
    full, stores = (full_p, full_o, full_e, full_s), (v_p, v_o, v_e, v_s)
    own = (own_p, own_o, own_e, own_s)
    ring = Ring(own, full, link_send, link_recv, twin_send, twin_recv)
    x, y = ring.x, ring.y
    first, second = x == 0, x == 1
    width = entry.shape[1]
    parts = 2

    barrier(list(ring.peers.values()))
    entry_copy = pltpu.make_async_copy(entry, v_x.at[0], x_sem.at[0])
    entry_copy.start()
    mine, beside, across, far = (x, y), (x, 1 - y), (1 - x, y), (1 - x, 1 - y)
    posted = {0: [], 1: []}

    def post(section, index, quarter, kind, peer):
        ring.send(index, quarter, kind, peer)
        posted[section].append((index, quarter, kind, peer))

    @pl.when(first)
    def _start_first():
        for index in range(CHUNKS):
            post(0, index, mine, 0, "x")
            post(0, index, mine, 1, "y")

    @pl.when(second)
    def _start_second():
        for index in range(CHUNKS):
            post(1, index, mine, 0, "x")

    def sync(section_first, section_second):
        pl.when(first)(section_first)
        pl.when(second)(section_second)

    def load(layer, weight):
        store, sems = stores[weight], load_sem.at[weight]
        whole = pltpu.make_async_copy(full[weight].at[layer], store, sems)

        @pl.when(x == layer)
        def _here():
            pltpu.make_async_copy(own[weight], store.at[y], sems).start()
            pltpu.make_async_copy(full[weight].at[layer, 1 - y], store.at[1 - y], sems).start()

        pl.when(x != layer)(whole.start)
        return whole

    def keep_own(weight, layer):
        copy = pltpu.make_async_copy(stores[weight].at[y], full[weight].at[layer, y], own_sem.at[weight])
        pl.when(x == layer)(copy.start)
        return lambda: pl.when(x == layer)(copy.wait)

    def complete(indices, *quarters):
        for index in indices:
            for quarter in quarters:
                ring.complete(index, quarter)

    def project_first():
        for index in range(3):
            ring.arrive(index, beside)
            ring.arrive(index, across)
        complete(range(3), beside)

    def project_second():
        for index in range(3):
            ring.arrive(index, across)
            post(1, index, across, 2, "y")
        for index in range(3):
            ring.arrive(index, far)
        complete(range(3), across, far)

    def mid_first():
        for index in (3, 4):
            ring.arrive(index, beside)
            ring.arrive(index, across)
        post(0, 4, across, 2, "y")

    def mid_second():
        for index in (3, 4):
            ring.arrive(index, across)
            post(1, index, across, 2, "y")

    def feed_first():
        for index in (5, 6, 7):
            ring.arrive(index, beside)
            ring.arrive(index, across)
            post(0, index, across, 2, "y")
        complete(range(3, 8), beside)

    def feed_second():
        for index in (5, 6, 7):
            ring.arrive(index, across)
            post(1, index, across, 2, "y")
        for index in range(4):
            post(1, index, mine, 1, "y")
        for index in range(3, 8):
            ring.arrive(index, far)
        complete(range(3, 8), across, far)

    def last_project_first():
        for index in (4, 5):
            ring.arrive(index, far)
            post(0, index, far, 3, "x")
        for index in range(3):
            ring.arrive(index, far)
        complete(range(3), across, far)

    def last_project_second():
        for index in range(3):
            ring.arrive(index, beside)
            post(1, index, beside, 3, "x")
        complete(range(3), beside)

    def last_mid_first():
        for index in (6, 7):
            ring.arrive(index, far)
            post(0, index, far, 3, "x")

    def last_mid_second():
        ring.arrive(3, beside)
        post(1, 3, beside, 3, "x")

    def last_feed_first():
        ring.arrive(3, far)
        complete(range(3, 8), across, far)

    def last_feed_second():
        for index in range(4, 8):
            ring.arrive(index, beside)
        complete(range(3, 8), beside)

    def run_project(layer):
        @pl.loop(0, LIVE // BLOCK)
        def _rows(step):
            rows = block_rows(step)
            shift_scale = dot_nn(one[rows], mods[layer, :, : 2 * width])
            unit, _ = normal(v_x[layer, rows].astype(f32))
            normed = (unit * (1.0 + shift_scale[:, width:]) + shift_scale[:, :width]).astype(bf16)
            v_normed[rows] = normed
            for part in range(parts):
                for kind in range(3):
                    out = dot_nn(normed, v_p[part, kind * width : (kind + 1) * width, :])
                    out = out + p_bias[layer, part, kind : kind + 1, :]
                    if kind < 2:
                        out = turn(out, cosine[rows], sine[rows])
                    v_heads[part, kind, rows] = out.astype(bf16)

    def run_attend(part):
        allowed = seg_column[...] == seg_row[...]

        @pl.loop(0, v_heads.shape[3] // LANES)
        def _pairs(pair):
            lanes = pl.ds(pl.multiple_of(pair * LANES, LANES), LANES)
            for start, size, mask in ((0, LONGEST, None), (LONGEST, LIVE - LONGEST, allowed)):
                rows = pl.ds(start, size)
                out, total = attend_block(
                    v_heads[part, 1, rows, lanes], v_heads[part, 0, rows, lanes], v_heads[part, 2, rows, lanes], mask
                )
                v_att[part, rows, lanes] = out.astype(bf16)
                v_tot[part, pair, :, rows] = total

    def run_feed(layer):
        @pl.loop(0, LIVE // BLOCK)
        def _rows(step):
            rows = block_rows(step)
            token = dot_nn(one[rows], mods[layer, :, 2 * width :])
            branch = o_bias[layer]
            for part in range(parts):
                branch = branch + dot_nn(v_att[part, rows], v_o[part])
            v_ba[rows] = branch.astype(bf16)
            middle = v_x[layer, rows].astype(f32) + token[:, :width] * branch
            v_mid[rows] = middle
            unit, _ = normal(middle)
            normed = unit * (1.0 + token[:, 2 * width : 3 * width]) + token[:, width : 2 * width]
            normed = normed.astype(bf16)
            v_nf[rows] = normed
            hidden = []
            for part in range(parts):
                act = dot_nn(normed, v_e[part]) + e_bias[layer, part]
                v_inner[part, rows] = act.astype(bf16)
                bend = jnp.tanh(GELU * act * (1.0 + 0.044715 * act * act))
                hidden.append((act * (0.5 + 0.5 * bend)).astype(bf16))
            branch = s_bias[layer]
            for part in range(parts):
                branch = branch + dot_nn(hidden[part], v_s[part])
            v_bf[rows] = branch.astype(bf16)
            v_x[layer + 1, rows] = (middle + token[:, 3 * width :] * branch).astype(bf16)

    def saves(layer):
        pairs = (
            (v_normed, normed_a), (v_heads, heads), (v_att, attended), (v_tot, totals), (v_mid, mid),
            (v_ba, branch_a), (v_nf, normed_f), (v_inner, inner), (v_bf, branch_f), (v_x.at[layer + 1], x_out),
        )
        return [pltpu.make_async_copy(a, b.at[layer], save_sem.at[i]) for i, (a, b) in enumerate(pairs)]

    for layer in range(2):
        if layer == 0:
            sync(project_first, project_second)
        else:
            sync(last_project_first, last_project_second)
        copy = load(layer, 0)
        if layer == 0:
            entry_copy.wait()
        else:
            for save in saved:
                save.wait()
        copy.wait()
        owned = [keep_own(0, layer)]
        run_project(layer)
        saved = saves(layer)
        saved[0].start()
        saved[1].start()
        if layer == 0:
            sync(mid_first, mid_second)
        else:
            sync(last_mid_first, last_mid_second)
        for part in range(parts):
            run_attend(part)
        saved[2].start()
        saved[3].start()
        if layer == 0:
            sync(feed_first, feed_second)
        else:
            sync(last_feed_first, last_feed_second)
        copies = [load(layer, weight) for weight in (1, 2, 3)]
        for copy in copies:
            copy.wait()
        owned += [keep_own(weight, layer) for weight in (1, 2, 3)]
        run_feed(layer)
        for done in owned:
            done()
        for save in saved[4:]:
            save.start()
    for save in saved:
        save.wait()

    def finish(section, quarters):
        ring.sent_all(posted[section])
        for quarter in quarters:
            for index in range(CHUNKS):
                ring.hand(index, quarter, ring.c).wait_send()

    sync(lambda: finish(0, (beside, across, far)), lambda: finish(1, (beside, across, far)))


def forward_both(own, entry, one, mods, p_bias, e_bias, o_bias, s_bias, cosine, sine, seg_row, seg_column):
    rows, width = entry.shape
    columns, hidden = own[0].shape[1], own[2].shape[1]
    pairs = columns // LANES
    vmem = pl.BlockSpec(memory_space=pltpu.VMEM)
    full = [shape_of((2, 2) + w.shape, bf16) for w in own]
    saved = [
        ((rows, width), bf16),
        ((2, 3, rows, columns), bf16),
        ((2, rows, columns), bf16),
        ((2, pairs, 2, rows), f32),
        ((rows, width), f32),
        ((rows, width), bf16),
        ((rows, width), bf16),
        ((2, rows, hidden), bf16),
        ((rows, width), bf16),
    ]
    outs = full + [shape_of((2,) + s, k) for s, k in saved] + [shape_of((2, rows, width), bf16)]
    return pl.pallas_call(
        forward_kernel,
        in_specs=[any_spec()] * 5 + [vmem] * 10,
        out_specs=[any_spec()] * len(outs),
        out_shape=outs,
        scratch_shapes=[pltpu.VMEM((2,) + w.shape, bf16) for w in own]
        + [pltpu.VMEM((3, rows, width), bf16)]
        + [pltpu.VMEM(s, k) for s, k in saved]
        + [
            pltpu.SemaphoreType.DMA((CHUNKS, 4)),
            pltpu.SemaphoreType.DMA((CHUNKS, 2, 2)),
            pltpu.SemaphoreType.DMA((CHUNKS, 2, 2)),
            pltpu.SemaphoreType.DMA((CHUNKS, 2, 2)),
            pltpu.SemaphoreType.DMA((4,)),
            pltpu.SemaphoreType.DMA((4,)),
            pltpu.SemaphoreType.DMA((1,)),
            pltpu.SemaphoreType.DMA((10,)),
        ],
        compiler_params=pltpu.CompilerParams(
            collective_id=1, has_side_effects=True, vmem_limit_bytes=VMEM_LIMIT
        ),
        cost_estimate=cost(2 * 2 * rows * 8 * width * width, 64 << 20),
        name="forward_both",
    )(*own, entry, one, mods, p_bias, e_bias, o_bias, s_bias, cosine, sine, seg_row, seg_column)


def weight_grad_split_kernel(core, left, right, send, keep):
    value = dot_tn(left[...].reshape(left.shape[-2:]), right[...].reshape(right.shape[-2:]))
    side = pl.program_id(0)

    @pl.when(side == 0)
    def _send():
        send[0] = value.astype(bf16)

    @pl.when(side == 1)
    def _keep():
        keep[0] = value.astype(bf16)


def weight_grad_kernel(left, right, out):
    value = dot_tn(left[...].reshape(left.shape[-2:]), right[...].reshape(right.shape[-2:]))
    out[0] = value.astype(bf16)


def weight_grad(core, left, right, parts):
    frames, columns = right.shape[-2:]
    kinds = right.shape[1] if right.ndim == 4 else 1
    left_rows = left.shape[-1]
    rows = kinds * left_rows
    estimate = cost(2 * frames * rows * columns * parts, 2 * parts * rows * columns + (6 << 20))
    if core is None:
        left_block = pl.BlockSpec(
            (1,) * (left.ndim - 2) + (frames, left_rows),
            (lambda p, k: (p, 0, 0)) if left.ndim == 3 else (lambda p, k: (0, 0)),
        )
        right_block = pl.BlockSpec(
            (1,) * (right.ndim - 2) + (frames, columns),
            {
                2: lambda p, k: (0, 0),
                3: lambda p, k: (p, 0, 0),
                4: lambda p, k: (p, k, 0, 0),
            }[right.ndim],
        )
        return pl.pallas_call(
            weight_grad_kernel,
            grid=(parts, kinds),
            in_specs=[left_block, right_block],
            out_specs=pl.BlockSpec((1, left_rows, columns), lambda p, k: (p, k, 0)),
            out_shape=shape_of((parts, rows, columns), bf16),
            compiler_params=params_of(2),
            cost_estimate=estimate,
            name="weight_grad",
        )(left, right)
    unit = left_rows // 2

    def unit_of(side, step, core_ref):
        half = jnp.where(side == 0, 1 - core_ref[0], core_ref[0])
        return half * kinds + step

    def left_map(side, part, step, core_ref):
        column = unit_of(side, step, core_ref) % 2
        return (part, 0, column) if left.ndim == 3 else (0, column)

    def right_map(side, part, step, core_ref):
        kind = unit_of(side, step, core_ref) // 2
        return {2: (0, 0), 3: (part, 0, 0), 4: (part, kind, 0, 0)}[right.ndim]

    def send_map(side, part, step, core_ref):
        return (
            jnp.where(side == 0, part, parts - 1),
            jnp.where(side == 0, step, kinds - 1),
            0,
        )

    def keep_map(side, part, step, core_ref):
        return jnp.where(side == 1, part, 0), jnp.where(side == 1, step, 0), 0

    return pl.pallas_call(
        weight_grad_split_kernel,
        grid_spec=pltpu.PrefetchScalarGridSpec(
            num_scalar_prefetch=1,
            grid=(2, parts, kinds),
            in_specs=[
                pl.BlockSpec((1,) * (left.ndim - 2) + (frames, unit), left_map),
                pl.BlockSpec((1,) * (right.ndim - 2) + (frames, columns), right_map),
            ],
            out_specs=[
                pl.BlockSpec((1, unit, columns), send_map),
                pl.BlockSpec((1, unit, columns), keep_map),
            ],
        ),
        out_shape=[shape_of((parts, rows // 2, columns), bf16)] * 2,
        compiler_params=params_of(3),
        cost_estimate=estimate,
        name="weight_grad",
    )(core, left, right)


def add_rounded(*terms):
    total = terms[0].astype(f32)
    for term in terms[1:]:
        total = total + term.astype(f32)
    return total.astype(bf16)


class Relay:
    x01, x10 = [(0, 2), (1, 3)], [(2, 0), (3, 1)]
    y0, y1 = [(0, 1), (1, 0)], [(2, 3), (3, 2)]

    def __init__(self):
        self.section = lax.axis_index("section")
        self.mp = lax.axis_index("mp")
        self.core = lax.axis_index("core")
        self.slot = self.section * 2 + self.mp
        self.parts = 2
        self.core_arg = self.core.astype(jnp.int32).reshape(1)

    def hop(self, values, pairs):
        return lax.ppermute(values, GROUP, pairs)

    def twin(self, values):
        return lax.ppermute(values, "core", [(0, 1), (1, 0)])

    def place(self, layer):
        return jnp.stack([(self.section == layer).astype(jnp.int32), self.core.astype(jnp.int32)])

    def order(self, values):
        return values

    unorder = order

    def own_cotangent(self, cotangent):
        shard = cotangent.shape[1]
        rest = LIVE - shard
        to_one = self.hop(cotangent[1], [(0, 1)])
        to_zero = self.hop(cotangent[0, :rest], [(1, 0)])
        to_two = self.hop(cotangent[2, :rest], [(3, 2)])
        natural = [
            jnp.concatenate([cotangent[0], to_zero], 0),
            jnp.concatenate([to_one, cotangent[1, :rest]], 0),
            jnp.concatenate([cotangent[2], to_two], 0),
        ]
        live = jnp.where(self.slot == 0, natural[0], jnp.where(self.slot == 1, natural[1], natural[2]))
        return jnp.where(self.slot < 3, live, jnp.zeros_like(live))

    def to_owners(self, rows, layer, shard):
        head, tail = rows[:shard], rows[shard:]
        pad = lambda v: jnp.concatenate([v, jnp.zeros((shard - v.shape[0], v.shape[1]), v.dtype)], 0)
        outs = []
        for source in range(3):
            got = None
            for mp_index, piece in ((0, head), (1, tail)):
                target = 2 * layer + mp_index
                if target == source:
                    value = jnp.where(self.slot == source, piece, jnp.zeros_like(piece))
                else:
                    value = self.hop(piece, [(source, target)])
                value = value if value.shape[0] == shard else pad(value)
                got = value if got is None else got + value
            outs.append(got)
        return jnp.stack(outs)

    def reduce_near(self, send, keep):
        received = self.twin(send)
        low = add_rounded(keep[0], received[0])
        high = add_rounded(keep[1], received[1])
        near = jnp.where(self.mp == 0, low, high)
        away = jnp.where(self.mp == 0, high, low)
        return near, self.hop(away, self.y0 + self.y1)

    def reduce_first(self, send, keep):
        total = add_rounded(*self.reduce_near(send, keep))
        return total, self.hop(total, self.x01)

    def reduce_last(self, second, send, keep):
        total = add_rounded(*self.reduce_near(send, keep))
        arrived = self.hop(total, self.x10)
        here = self.section == 0
        own = jnp.where(here, total, second[0])
        other = jnp.where(here, arrived, second[1])
        summed = lax.psum(add_rounded(own, other), "z")
        return lax.all_gather(summed, "core", axis=0, tiled=True).astype(f32)


class General:
    def __init__(self, sections, mps):
        self.sections, self.mps = sections, mps
        self.section = lax.axis_index("section")
        self.mp = lax.axis_index("mp")
        self.slot = self.section * mps + self.mp
        self.parts = mps
        self.core_arg = None

    def place(self, layer):
        return jnp.zeros((2,), jnp.int32)

    def gather(self, weights):
        lists = [[] for _ in range(self.sections)]
        for weight in weights:
            every = lax.all_gather(weight, GROUP, axis=0, tiled=False)
            for layer in range(self.sections):
                lists[layer].append(tuple(every[layer * self.mps + part] for part in range(self.mps)))
        return lists

    def order(self, values):
        return values

    unorder = order

    def own_cotangent(self, cotangent):
        every = lax.all_gather(cotangent, "mp", axis=1, tiled=True)
        count = cotangent.shape[0]
        live = lax.dynamic_index_in_dim(every, jnp.minimum(self.slot, count - 1), 0, False)[:LIVE]
        return jnp.where(self.slot < count, live, jnp.zeros_like(live))

    def to_owners(self, rows, layer, shard):
        every = lax.all_gather(rows, GROUP, axis=0, tiled=False)[:3]
        padded = jnp.pad(every, ((0, 0), (0, shard * self.mps - rows.shape[0]), (0, 0)))
        return lax.dynamic_slice_in_dim(padded, self.mp * shard, shard, 1)

    def reduce_first(self, grads):
        return grads

    def reduce_last(self, second, grads):
        both = lax.psum(jnp.stack([grads, second]), ("section", "mp", "z", "core"))
        mine = lax.dynamic_index_in_dim(both, self.section, 0, False)
        return lax.dynamic_index_in_dim(mine, self.mp, 0, False).astype(f32)


def sinusoid(step_values, table_width):
    half_count = table_width // 2
    log_rate = math.log(10000.0) / (half_count - 1)
    frequency = jnp.exp(jnp.arange(half_count, dtype=f32) * -log_rate)
    angles = step_values.astype(f32)[:, None] * frequency[None, :]
    return jnp.concatenate([jnp.sin(angles), jnp.cos(angles)], 1)


def roll_rows(rows, start):
    return lax.dynamic_slice_in_dim(jnp.concatenate([rows, rows], 0), start, rows.shape[0], 0)


def on_device(
    frame_features,
    clip_lengths,
    audio_drop,
    text_drop,
    timesteps,
    cotangent,
    embed_weight,
    embed_bias,
    time_hidden_weight,
    time_hidden_bias,
    time_output_weight,
    time_output_bias,
    modulate_weight,
    modulate_bias,
    project_weight,
    project_bias,
    output_weight,
    output_bias,
    expand_weight,
    expand_bias,
    shrink_weight,
    shrink_bias,
):
    micro_count, frames, channels = frame_features.shape
    clip_count = clip_lengths.shape[2]
    width = cotangent.shape[2]
    shard = cotangent.shape[1]
    sections, mps = lax.axis_size("section"), lax.axis_size("mp")
    replicas = lax.axis_size("z") * lax.axis_size("core")
    group_size = sections * mps
    if sections == 2 and mps == 2 and micro_count == 3:
        net = Relay()
    else:
        net = General(sections, mps)
    parts, section, mp_index = net.parts, net.section, net.mp
    everyone = ("section", "mp", "z", "core")

    head_columns = project_weight.shape[3]
    project_own = jnp.transpose(project_weight[0], (1, 0, 2)).reshape(3 * width, head_columns)
    own_weights = (project_own, output_weight[0], expand_weight[0], shrink_weight[0])
    weights = None if isinstance(net, Relay) else net.gather(own_weights)

    small = (
        jnp.concatenate([project_bias[0].reshape(-1), expand_bias[0]]),
        jnp.concatenate([output_bias[0], shrink_bias[0]]),
    )
    shared_bias = lax.all_gather(jnp.concatenate(small), GROUP, axis=0, tiled=False).astype(f32)
    shared_bias = shared_bias.reshape(sections, mps, -1)
    split_bias = 3 * head_columns
    hidden_columns = expand_bias.shape[1]
    project_biases, expand_biases, output_biases, shrink_biases = [], [], [], []
    for layer in range(sections):
        one_layer = shared_bias[layer]
        project_biases.append(net.order(one_layer[:, :split_bias].reshape(mps, 3, head_columns)))
        expand_biases.append(
            net.order(one_layer[:, split_bias : split_bias + hidden_columns].reshape(mps, 1, hidden_columns))
        )
        tail = one_layer[0, split_bias + hidden_columns :]
        output_biases.append(tail[:width][None])
        shrink_biases.append(tail[width:][None])
    embed_full = lax.all_gather(
        jnp.concatenate([embed_weight, embed_bias[None]], 0), "mp", axis=1, tiled=True
    )
    embed_matrix, embed_offset = embed_full[:channels], embed_full[channels:].astype(f32)

    own_clips = micro_count * clip_count
    every_step = lax.all_gather(timesteps.reshape(-1), ("z", "core"), axis=0, tiled=True)
    table = sinusoid(every_step, time_hidden_weight.shape[0])
    hidden_pre = dot_split(table, time_hidden_weight) + time_hidden_bias.astype(f32)
    inner_time, inner_pull = jax.vjp(jax.nn.silu, hidden_pre)
    time_embed = dot_split(inner_time, time_output_weight) + time_output_bias.astype(f32)
    activated, silu_pull = jax.vjp(jax.nn.silu, time_embed)
    replica = lax.axis_index("z") * lax.axis_size("core") + lax.axis_index("core")
    activated_own = lax.dynamic_slice_in_dim(activated, replica * own_clips, own_clips, 0)
    modulate = jnp.transpose(modulate_weight[0], (1, 0, 2))
    high, low = split_rows(activated_own)
    both = jnp.einsum(
        "cd,jde->jce", jnp.concatenate([high, low], 0), modulate, preferred_element_type=f32
    )
    modulation = both[:, :own_clips] + both[:, own_clips:] + modulate_bias[0].astype(f32)[:, None]
    modulation = lax.all_gather(modulation, GROUP, axis=0, tiled=False)

    buffer = jnp.minimum(net.slot, micro_count - 1)
    pick = lambda values: lax.dynamic_index_in_dim(values, buffer, 0, False)
    lengths = pick(clip_lengths)[0]
    ends = jnp.cumsum(lengths)
    starts = ends - lengths
    longest = jnp.argmax(lengths)
    first = jnp.sum(jnp.where(jnp.arange(clip_count) == longest, starts, 0))
    frame_index = jnp.arange(LIVE, dtype=jnp.int32)
    frame_index = jnp.where(frame_index + first >= LIVE, frame_index + first - LIVE, frame_index + first)
    member = (frame_index[:, None] >= starts[None]) & (frame_index[:, None] < ends[None])
    onehot = member.astype(f32)
    position = jnp.sum(jnp.where(member, frame_index[:, None] - starts[None], 0), 1).astype(f32)
    segment = jnp.sum(jnp.where(member, jnp.arange(clip_count)[None], 0), 1).astype(f32)
    one = jnp.concatenate([onehot, onehot], 1).astype(bf16)
    seg_row, seg_column = segment[None, LONGEST:], segment[LONGEST:, None]
    lane = jnp.arange(LANES)
    inverse = 1.0 / 10000.0 ** ((lane % HEAD // 2).astype(f32) * 2.0 / HEAD)
    angles = position[:, None] * inverse[None]
    cosine = jnp.cos(angles)
    sine = jnp.sin(angles) * jnp.where(lane % 2 == 0, -1.0, 1.0)[None]

    columns = jnp.arange(channels)
    audio_columns = ((columns >= MEL) & (columns < 2 * MEL)).astype(f32)
    text_columns = (columns >= 2 * MEL).astype(f32)
    audio_keep = jnp.sum(onehot * (1 - pick(audio_drop)).astype(f32), 1)
    text_keep = jnp.sum(onehot * (1 - pick(text_drop)).astype(f32), 1)
    factor = (
        (1.0 - audio_columns - text_columns)[None]
        + audio_keep[:, None] * audio_columns[None]
        + text_keep[:, None] * text_columns[None]
    )
    masked = roll_rows(pick(frame_features)[:LIVE], first) * factor.astype(bf16)
    entry = (dot_nn(masked, embed_matrix) + embed_offset).astype(bf16)

    modulation = modulation.reshape(sections, mps, 6, micro_count, clip_count, -1)
    modulation = lax.dynamic_index_in_dim(modulation, buffer, 3, False)
    modulation = jnp.transpose(modulation, (0, 3, 2, 1, 4)).reshape(sections, clip_count, 6 * width)
    mod_high, mod_low = split_rows(modulation)
    mods = jnp.concatenate([mod_high, mod_low], 1)

    cot_rows = roll_rows(net.own_cotangent(cotangent), first)

    stream, kept, outputs = entry, [], []
    if isinstance(net, Relay):
        saved = forward_both(
            own_weights, entry, one, mods, jnp.stack(project_biases), jnp.stack(expand_biases),
            jnp.stack(output_biases), jnp.stack(shrink_biases), cosine, sine, seg_row, seg_column,
        )
        full, saved = saved[:4], saved[4:]
        streams_in = (entry, saved[9][0])
        for layer in range(2):
            kept.append((streams_in[layer],) + tuple(value[layer] for value in saved[:9]))
            outputs.append(roll_rows(saved[9][layer], LIVE - first))
        weights = [[tuple(w[layer, part] for part in range(2)) for w in full] for layer in range(2)]
    for layer in range(0 if isinstance(net, Relay) else 2):
        place, mod = net.place(layer), mods[layer]
        project_refs, out_refs, in_refs, shrink_refs = weights[layer]
        normed_a, heads = project(
            place, stream, one, mod[:, : 2 * width], project_biases[layer], cosine, sine,
            project_refs, parts, head_columns,
        )
        attended, totals = attend(seg_row, seg_column, heads)
        mid, branch_a, normed_f, inner, branch_f, stream_out = feed(
            place, stream, attended, one, mod[:, 2 * width :],
            output_biases[layer], expand_biases[layer], shrink_biases[layer],
            out_refs, in_refs, shrink_refs,
        )
        kept.append((stream, normed_a, heads, attended, totals, mid, branch_a, normed_f, inner, branch_f))
        outputs.append(roll_rows(stream_out, LIVE - first))
        stream = stream_out

    grad, gradients, second = cot_rows, [None, None], None
    clip_sums, row_totals, inner_totals, head_totals = [None, None], [None, None], [None, None], [None, None]
    reduced = []
    for layer in (1, 0):
        place, mod = net.place(layer), mods[layer]
        project_refs, out_refs, in_refs, shrink_refs = weights[layer]
        x, normed_a, heads, attended, totals, mid, branch_a, normed_f, inner, branch_f = kept[layer]
        gf, hidden, dinner, ga, datt, gmid, dmod_f, row_sums, inner_sums = feed_back(
            place, grad, inner, mid, branch_a, branch_f, one, mod[:, 2 * width :],
            out_refs, in_refs, shrink_refs, head_columns,
        )
        partials = [None] * 4
        partials[3] = weight_grad(net.core_arg, hidden, gf, parts)
        partials[2] = weight_grad(net.core_arg, normed_f, dinner, parts)
        partials[1] = weight_grad(net.core_arg, attended, ga, parts)
        dheads = attend_back(seg_row, seg_column, cosine, sine, heads, attended, datt, totals)
        partials[0] = weight_grad(net.core_arg, normed_a, dheads, parts)
        grad, dmod_a, head_sums = project_back(
            place, gmid, x, dheads, one, mod[:, width : 2 * width], project_refs
        )
        gradients[layer] = roll_rows(grad, LIVE - first)
        clip_sums[layer] = jnp.concatenate([dmod_a, dmod_f], 0)[:, :clip_count]
        row_totals[layer] = jnp.sum(row_sums[:, :clip_count], 1)
        inner_totals[layer] = net.unorder(jnp.sum(inner_sums[:, :clip_count], 1))
        head_totals[layer] = net.unorder(jnp.sum(head_sums[:, :, :clip_count], 2))
        if layer == 1:
            second = [net.reduce_first(*(p if isinstance(p, (list, tuple)) else (p,))) for p in partials]
        else:
            reduced = [
                net.reduce_last(s, *(p if isinstance(p, (list, tuple)) else (p,)))
                for s, p in zip(second, partials)
            ]

    row_start = mp_index * shard
    shard_rows = row_start + jnp.arange(shard, dtype=jnp.int32)
    padding = (shard_rows >= LIVE)[None, :, None]
    shard_mel = lax.dynamic_slice_in_dim(frame_features, row_start, shard, 1)[:, :, :MEL]
    pad_entry = (
        jnp.einsum("mfe,ed->mfd", shard_mel, embed_matrix[:MEL], preferred_element_type=f32)
        + embed_offset
    ).astype(bf16)
    streams = [net.to_owners(outputs[layer], layer, shard) for layer in range(2)]
    stream_grads = [net.to_owners(gradients[layer], layer, shard) for layer in range(2)]
    here = section == 0
    stream_all = jnp.where(padding, pad_entry, jnp.where(here, streams[0], streams[1]))[None]
    grad_all = jnp.where(padding, cotangent, jnp.where(here, stream_grads[0], stream_grads[1]))
    grad_all = grad_all.astype(f32)[None]

    pad_grad = jnp.where(padding & here, cotangent, jnp.zeros_like(cotangent))
    embed_partial = dot_tn(masked, grad)
    mel_partial = jnp.einsum("mfe,mfd->ed", shard_mel, pad_grad, preferred_element_type=f32)
    embed_partial = jnp.concatenate([embed_partial[:MEL] + mel_partial, embed_partial[MEL:]], 0)
    embed_sum = jnp.sum(grad.astype(f32), 0) + jnp.sum(pad_grad.astype(f32), (0, 1))
    embed_near = lax.psum_scatter(
        embed_partial.astype(bf16), "mp", scatter_dimension=1, tiled=True
    )
    embed_weight_grad = lax.psum(embed_near, ("section", "z", "core")).astype(f32)

    pieces = [embed_sum]
    for layer in range(2):
        pieces += [
            row_totals[layer].reshape(-1),
            inner_totals[layer].reshape(-1),
            head_totals[layer].reshape(-1),
        ]
    vector = lax.psum(jnp.concatenate(pieces), everyone)
    embed_bias_grad = lax.dynamic_slice_in_dim(vector[:width], mp_index * (width // mps), width // mps, 0)
    per_layer = vector[width:].reshape(2, -1)
    layer_vector = jnp.where(here, per_layer[0], per_layer[1])
    shrink_bias_grad = layer_vector[:width]
    output_bias_grad = layer_vector[width : 2 * width]
    inner_end = 2 * width + mps * hidden_columns
    expand_bias_grad = lax.dynamic_index_in_dim(
        layer_vector[2 * width : inner_end].reshape(mps, -1), mp_index, 0, False
    )
    project_bias_grad = lax.dynamic_index_in_dim(
        layer_vector[inner_end:].reshape(mps, 3, -1), mp_index, 0, False
    )

    clip_all = jnp.stack(clip_sums)
    clip_all = lax.all_gather(clip_all, GROUP, axis=0, tiled=False)[:micro_count]
    clip_own = lax.dynamic_index_in_dim(clip_all, section, 1, False)
    clip_own = lax.dynamic_slice_in_dim(clip_own, mp_index * (width // mps), width // mps, 3)
    clip_own = jnp.transpose(clip_own, (1, 0, 2, 3)).reshape(6, own_clips, -1)
    clip_every = lax.all_gather(clip_own, ("z", "core"), axis=1, tiled=True)
    modulate_bias_grad = jnp.sum(clip_every, 1)
    clip_low = clip_every.astype(bf16)
    modulate_weight_grad = jnp.einsum(
        "cd,jce->jde", activated.astype(bf16), clip_low, preferred_element_type=f32
    )
    activated_part = jnp.einsum("jce,jde->cd", clip_low, modulate, preferred_element_type=f32)
    activated_grad = lax.psum(activated_part, GROUP)
    time_grad = silu_pull(activated_grad)[0]
    time_low = time_grad.astype(bf16)
    time_output_grad = dot_tn(inner_time.astype(bf16), time_low)
    hidden_grad = inner_pull(dot_nt(time_low, time_output_weight))[0]
    time_hidden_grad = dot_tn(table.astype(bf16), hidden_grad.astype(bf16))

    project_grad = jnp.transpose(reduced[0].reshape(3, width, head_columns), (1, 0, 2))
    return (
        stream_all,
        grad_all,
        embed_weight_grad,
        embed_bias_grad,
        time_hidden_grad,
        jnp.sum(hidden_grad, 0),
        time_output_grad,
        jnp.sum(time_grad, 0),
        jnp.transpose(modulate_weight_grad, (1, 0, 2))[None],
        modulate_bias_grad[None],
        project_grad[None],
        project_bias_grad[None],
        reduced[1][None],
        output_bias_grad[None],
        reduced[2][None],
        expand_bias_grad[None],
        reduced[3][None],
        shrink_bias_grad[None],
    )


def solution(mesh):
    sections, replicas, mps = (mesh.shape[name] for name in ("section", "dp", "mp"))
    fine = Mesh(mesh.devices.reshape(sections, replicas // 2, 2, mps), ("section", "z", "core", "mp"))
    dp = ("z", "core")
    return jax.shard_map(
        on_device,
        mesh=fine,
        in_specs=(
            P(None, dp, None),
            P(None, dp, None),
            P(None, dp, None),
            P(None, dp, None),
            P(None, dp, None),
            P(None, ("z", "core", "mp"), None),
            P(None, "mp"),
            P("mp"),
            P(),
            P(),
            P(),
            P(),
            P("section", None, None, "mp"),
            P("section", None, "mp"),
            P("section", None, None, "mp"),
            P("section", None, "mp"),
            P("section", "mp", None),
            P("section", None),
            P("section", None, "mp"),
            P("section", "mp"),
            P("section", "mp", None),
            P("section", None),
        ),
        out_specs=(
            P("section", None, ("z", "core", "mp"), None),
            P("section", None, ("z", "core", "mp"), None),
            P(None, "mp"),
            P("mp"),
            P(),
            P(),
            P(),
            P(),
            P("section", None, None, "mp"),
            P("section", None, "mp"),
            P("section", None, None, "mp"),
            P("section", None, "mp"),
            P("section", "mp", None),
            P("section", None),
            P("section", None, "mp"),
            P("section", "mp"),
            P("section", "mp", None),
            P("section", None),
        ),
        check_vma=False,
    )
```
